256 devices in a mesh: grid: 64 (over z, y, core), chan: 4 (over x).
Axes of the slice: x: 4, y: 4, z: 8, core: 2. Of those that a mesh axis runs over, the one named last changes fastest.
Arguments:
- profiles: bfloat16 [65536, 274], P('grid'), may hold values from -6 to 6
- owner_block: int32 [262144, 1], P(('grid', 'chan')), may hold values from 0 to 63; in each aligned block of 1024 rows (0 to 1023, 1024 to 2047, ...) at most 32 rows name the same one
- column_offset: int32 [262144], P(('grid', 'chan')), may hold values from 0 to 1023
- observed: float32 [262144, 384], P(('grid', 'chan')), may hold values from -8 to 8
- sigma: float32 [384], replicated, may hold values from 0.5 to 2
- qc_flags: int32 [262144, 384], P(('grid', 'chan')), may hold values 0 or 1
- w_first: bfloat16 [274, 512], replicated, may hold values from -0.375 to 0.375
- w_second: bfloat16 [512, 512], replicated, may hold values from -0.25 to 0.25
- w_third: bfloat16 [512, 384], replicated, may hold values from -0.25 to 0.25
Outputs:
- grad_profiles: float32 [65536, 274], P(('grid', 'chan'))
The draws below stay inside these ranges and needn't reach their ends.
Inputs may be any that keep to these rules, and one draw needn't show every extreme that they name: `owner_block`: in the rows of one device (aligned blocks of 1024 rows) no value appears more than 32 times, and some value appears exactly 32 times.
All inputs are finite; a program needn't handle non-finite values. No bound on the sum of `qc_flags` on one device may be relied on, other than what follows from the above.
Results may differ from the reference program's by a relative error of at most 0.0063.
Values may be sent and summed in bfloat16 or wider, within the bound.
No kernel may reach another device: no remote copies, remote signals or barrier semaphores. Data moves between devices by JAX's collectives and lax.ppermute only.
A program may use at most 128 MiB of HBM per device.

```python
import math
import jax
import jax.numpy as jnp
import numpy as np

PROF = 274
HID = 512
CHANS = 384
S_DEV = 1024
COL_DEV = 1024
CAP = 32
SOUNDINGS = 262144
NCOL = 65536
N_GRID = 64


def set_ends(values, key, smallest, largest):
    longest = values.shape.index(max(values.shape))
    spots = []
    for shift in (0, 1):
        where = [jax.random.randint(jax.random.fold_in(key, axis), (), 0, length) for axis, length in enumerate(values.shape)]
        where[longest] = (where[longest] + shift) % values.shape[longest]
        spots.append(tuple(where))
    return values.at[spots[0]].set(smallest).at[spots[1]].set(largest)


def shard_levels(own_key, extent, pieces, low, largest):
    def one(axis_at, blocks):
        heights = jax.random.uniform(jax.random.fold_in(jax.random.fold_in(own_key, 6), axis_at), (blocks,), jnp.float32, low / len(pieces), largest / len(pieces))
        return jnp.repeat(jnp.exp(heights), extent[axis_at] // blocks).reshape((-1,) + (1,) * (len(extent) - axis_at - 1))

    gain = one(*pieces[0])
    for cut in pieces[1:]:
        gain = gain * one(*cut)
    return gain


def deal_out(key, own, number, rows, count, top, reach, skew):
    sequence = jax.random.permutation(key, count)
    crowded, ordinary = load_shares(count, rows * top, reach, skew, True), load_shares(count, rows * top, reach, skew, False)
    places = jnp.arange(count)

    def named(tallies, rotation):
        used = int((tallies > 0).sum())
        fixed = max(1, used // 4)
        shifted = fixed + (places - fixed + rotation * (used - fixed)) % max(1, count - fixed)
        return jnp.zeros((count,), jnp.int32).at[sequence[jnp.where(places < fixed, places, shifted)]].set(jnp.asarray(tallies, jnp.int32))

    tallies = jnp.where(number % 4 == 0, named(crowded, number // 4), named(ordinary, number - number // 4 - 1))
    mixed = jax.random.permutation(jax.random.fold_in(own, 3), count)
    giver, receiver = mixed[0:count // 2 * 2:2], mixed[1:count // 2 * 2:2]
    margin = jnp.minimum(tallies[giver] - 1, reach - tallies[receiver]) // 2
    margin = jnp.where((giver == sequence[0]) | (receiver == sequence[0]) | (tallies[receiver] == 0), 0, jnp.maximum(margin, 0))
    shifted = jax.random.randint(jax.random.fold_in(own, 4), (count // 2,), 0, 1 << 20) % (margin + 1)
    tallies = tallies.at[giver].add(-shifted).at[receiver].add(shifted)
    members = jnp.searchsorted(jnp.cumsum(tallies), jnp.arange(rows * top), side="right").astype(jnp.int32)
    table = members.reshape(top, rows).T
    table = table[jax.random.permutation(jax.random.fold_in(own, 1), rows)]
    rotation = jax.random.randint(jax.random.fold_in(own, 2), (rows, 1), 0, top)
    return jnp.take_along_axis(table, (jnp.arange(top)[None, :] + rotation) % top, axis=1)


def load_shares(number_of, total, reach, slope, full):
    loads = [(1 << 20) // math.isqrt(grade ** slope) + 1 for grade in range(1, number_of + 1)]
    largest = reach if full else min(reach, max(-(-total // number_of), total * loads[0] // sum(loads)))
    least = 1 if total - largest >= number_of - 1 else 0
    holding, rest = [largest] + [least] * (number_of - 1), total - largest - least * (number_of - 1)
    while rest > 0:
        movable = [i for i in range(1, number_of) if holding[i] < largest] or [i for i in range(1, number_of) if holding[i] < reach]
        whole, budget = sum([loads[i] for i in movable]), rest
        for i in movable:
            addition = min(reach - holding[i], max(1, budget * loads[i] // whole), rest)
            holding[i] = holding[i] + addition
            rest = rest - addition
    return np.array(holding)


def gaussian(stream_key, extent, deviation, bound, cuts=(), dtype=jnp.bfloat16):
    array = deviation * jax.random.normal(stream_key, extent, jnp.float32)
    if cuts:
        array = array * shard_levels(stream_key, extent, cuts, -0.22, 0.18)
    return jnp.clip(array, -bound, bound).astype(dtype)


def setup_inputs(seed: int = 0) -> dict:
    seeds = jax.random.split(jax.random.key(seed), 10)
    profiles = gaussian(seeds[0], (NCOL, PROF), 1.0, 6.0, ((0, 64),))
    owner_block_keys = jax.random.split(jax.random.fold_in(seeds[1], 1), SOUNDINGS // S_DEV)
    owner_block_turns = jax.random.permutation(jax.random.fold_in(seeds[1], 3), SOUNDINGS // S_DEV)
    owner_block = jax.vmap(lambda own, number: deal_out(jax.random.fold_in(seeds[1], 2), own, number, S_DEV, N_GRID, 1, CAP, 2))(owner_block_keys, owner_block_turns).reshape((SOUNDINGS, 1))
    column_offset = set_ends(jax.random.randint(seeds[2], (SOUNDINGS,), 0, COL_DEV), jax.random.fold_in(seeds[2], 1), 0, COL_DEV - 1).astype(jnp.int32)
    observed = gaussian(seeds[3], (SOUNDINGS, CHANS), 1.5, 8.0, ((0, 256),), jnp.float32)
    sigma = jnp.clip(jnp.exp(jax.random.uniform(seeds[4], (CHANS,), jnp.float32, math.log(0.5), math.log(2.0))), 0.5, 2.0)
    qc_flags = set_ends((jax.random.randint(seeds[5], (SOUNDINGS, CHANS), 0, 10) < 9).astype(jnp.int32), jax.random.fold_in(seeds[5], 1), 0, 1)
    w_first = gaussian(seeds[6], (PROF, HID), PROF ** -0.5, 0.375)
    w_second = gaussian(seeds[7], (HID, HID), HID ** -0.5, 0.25)
    w_third = gaussian(seeds[8], (HID, CHANS), HID ** -0.5, 0.25)
    return dict(profiles=profiles, owner_block=owner_block, column_offset=column_offset, observed=observed, sigma=sigma, qc_flags=qc_flags, w_first=w_first, w_second=w_second, w_third=w_third)


def reference(profiles, owner_block, column_offset, observed, sigma, qc_flags, w_first, w_second, w_third):
    column = owner_block[:, 0] * COL_DEV + column_offset
    inputs = jnp.take(profiles, column, axis=0)
    first = jnp.tanh(jnp.dot(inputs, w_first, preferred_element_type=jnp.float32)).astype(jnp.bfloat16)
    second = jnp.tanh(jnp.dot(first, w_second, preferred_element_type=jnp.float32)).astype(jnp.bfloat16)
    evolved = jnp.dot(second, w_third, preferred_element_type=jnp.float32)
    departure = (evolved - observed) / sigma
    grad_sim = (qc_flags.astype(jnp.float32) * jnp.clip(departure, -1.5, 1.5) / sigma).astype(jnp.bfloat16)
    second_f = second.astype(jnp.float32)
    first_f = first.astype(jnp.float32)
    back_two = jnp.dot(grad_sim, w_third.T, preferred_element_type=jnp.float32)
    grad_second = (back_two * (1.0 - second_f * second_f)).astype(jnp.bfloat16)
    back_one = jnp.dot(grad_second, w_second.T, preferred_element_type=jnp.float32)
    grad_first = (back_one * (1.0 - first_f * first_f)).astype(jnp.bfloat16)
    grad_inputs = jnp.dot(grad_first, w_first.T, preferred_element_type=jnp.float32)
    return jax.ops.segment_sum(grad_inputs, column, num_segments=NCOL)
```

```python
import functools

import jax
import jax.numpy as jnp
from jax import lax
from jax.experimental import pallas as pl
from jax.experimental.pallas import tpu as pltpu
from jax.sharding import PartitionSpec as P

LANES = 128
PACK = 4
SPAN = LANES // PACK
F32 = jnp.float32
BF16 = jnp.bfloat16
NT = (((1,), (1,)), ((), ()))


def iota(shape, axis):
    return lax.broadcasted_iota(jnp.int32, shape, axis)


def nn(a, b):
    return jnp.dot(a, b, preferred_element_type=F32)


def nt(a, b):
    return lax.dot_general(a, b, NT, preferred_element_type=F32)


def call(kernel, out, args, vmem=48, **kw):
    return pl.pallas_call(
        kernel,
        out_shape=out,
        compiler_params=pltpu.CompilerParams(vmem_limit_bytes=vmem * 2**20),
        **kw,
    )(*args)


def slots_kernel(owners, cap, target_ref, offset_ref, place_ref, request_ref):
    tiles = target_ref.shape[0]
    target = target_ref[...]
    offset = offset_ref[...]
    hot = jnp.concatenate(
        [
            jnp.where(iota((owners, LANES), 0) == target[r : r + 1, :], 1.0, 0.0)
            for r in range(tiles)
        ],
        axis=1,
    )
    upper = jnp.where(iota((256, 256), 0) <= iota((256, 256), 1), 1.0, 0.0).astype(BF16)
    carry = jnp.zeros((owners, 1), F32)
    slots = []
    for b in range(tiles * LANES // 256):
        part = hot[:, b * 256 : (b + 1) * 256]
        count = nn(part.astype(BF16), upper) + carry
        carry = count[:, 255:256]
        slots.append(jnp.sum(part * (count - 1.0), axis=0, keepdims=True))
    slot = jnp.concatenate(slots, axis=1)
    high = offset // 32
    low = offset - high * 32
    flat = lambda a: jnp.concatenate([a[r : r + 1, :] for r in range(tiles)], axis=1)
    at_slot = jnp.where(
        iota((cap, tiles * LANES), 0).astype(F32) == slot, 1.0, 0.0
    )
    hot = hot.astype(BF16)
    table_high = nt(hot, (at_slot * flat(high.astype(F32))).astype(BF16))
    table_low = nt(hot, (at_slot * flat(low.astype(F32))).astype(BF16))
    filled = nt(hot, at_slot.astype(BF16))
    request_ref[...] = jnp.where(
        filled > 0.5, table_high * 32.0 + table_low, -1.0
    ).astype(jnp.int32)
    slot8 = jnp.concatenate(
        [slot[:, r * LANES : (r + 1) * LANES] for r in range(tiles)], axis=0
    )
    place_ref[...] = target * cap + slot8.astype(jnp.int32)


def gather_kernel(cap, wanted_ref, profiles_ref, out_ref, table):
    cols, width = profiles_ref.shape
    rest = width - 2 * LANES
    table[:, 2 * LANES :] = jnp.zeros((cols, LANES), BF16)
    table[:, : 2 * LANES] = profiles_ref[:, : 2 * LANES]
    table[:, 2 * LANES : width] = profiles_ref[:, 2 * LANES : width]
    sources = wanted_ref.shape[0]
    wanted = wanted_ref[...].astype(F32).T
    group = 16
    column = iota((cap, cols), 1).astype(F32)
    eighth = cap // PACK
    for s in range(0, sources, group):
        pick = jnp.concatenate(
            [
                jnp.where(wanted[:, s + j : s + j + 1] == column, 1.0, 0.0).astype(BF16)
                for j in range(group)
            ],
            axis=0,
        )
        rows = nn(pick, table[...]).reshape(group, cap, 3 * LANES)
        tail = rows[:, :, 2 * LANES :]
        packed = tail[:, :eighth, :]
        for g in range(1, PACK):
            packed = packed + pltpu.roll(
                tail[:, g * eighth : (g + 1) * eighth, :], g * SPAN, 2
            )
        out_ref[s : s + group, :cap, :] = rows[:, :, :LANES].astype(BF16)
        out_ref[s : s + group, cap : 2 * cap, :] = rows[:, :, LANES : 2 * LANES].astype(BF16)
        out_ref[s : s + group, 2 * cap :, :] = packed.astype(BF16)


def network_kernel(
    cap,
    place_ref,
    arrived_ref,
    observed_ref,
    flags_ref,
    sigma_ref,
    w1_ref,
    w2_ref,
    w3_ref,
    out_ref,
    main,
    w1_tail,
    grad_main,
    grad_tail,
):
    step = pl.program_id(0)
    owners = arrived_ref.shape[0]
    slots = owners * cap
    eighth = cap // PACK
    width, hidden = w1_ref.shape
    rest = width - 2 * LANES
    block = observed_ref.shape[0]

    @pl.when(step == 0)
    def _():
        main[:, :LANES] = arrived_ref[:, :cap, :].reshape(slots, LANES)
        main[:, LANES:] = arrived_ref[:, cap : 2 * cap, :].reshape(slots, LANES)
        tail = jnp.concatenate(
            [w1_ref[2 * LANES :, :].astype(F32), jnp.zeros((SPAN - rest, hidden), F32)], axis=0
        )
        w1_tail[...] = jnp.concatenate([tail] * PACK, axis=0).astype(BF16)

    place = place_ref[...]
    mine = place_ref[pl.ds(step * (block // LANES), block // LANES), :]
    column = jnp.concatenate(
        [
            jnp.broadcast_to(mine[r : r + 1, :], (LANES, LANES)).astype(F32).T
            for r in range(block // LANES)
        ],
        axis=0,
    ).astype(jnp.int32)[:, :1]
    slot = column & (cap - 1)
    pick = jnp.where(column == iota((block, slots), 1), 1.0, 0.0).astype(BF16)
    packed_at = (column // cap) * eighth + (slot & (eighth - 1))
    pick_tail = jnp.where(packed_at == iota((block, owners * eighth), 1), 1.0, 0.0).astype(BF16)
    in_span = iota((block, LANES), 1) // SPAN == slot // eighth

    inputs = nn(pick, main[...]).astype(BF16)
    packed = arrived_ref[:, 2 * cap :, :].reshape(owners * eighth, LANES)
    inputs_tail = jnp.where(in_span, nn(pick_tail, packed), 0.0).astype(BF16)
    first = jnp.tanh(nn(inputs, w1_ref[: 2 * LANES, :]) + nn(inputs_tail, w1_tail[...])).astype(BF16)
    second = jnp.tanh(nn(first, w2_ref[...])).astype(BF16)
    evolved = nn(second, w3_ref[...])
    inverse = 1.0 / sigma_ref[...]
    departure = (evolved - observed_ref[...]) * inverse
    grad_sim = (
        flags_ref[...].astype(F32) * jnp.clip(departure, -1.5, 1.5) * inverse
    ).astype(BF16)
    second_f = second.astype(F32)
    grad_second = (nt(grad_sim, w3_ref[...]) * (1.0 - second_f * second_f)).astype(BF16)
    first_f = first.astype(F32)
    grad_first = (nt(grad_second, w2_ref[...]) * (1.0 - first_f * first_f)).astype(BF16)
    here = pl.ds(pl.multiple_of(step * block, block), block)
    grad_main[here, :] = nt(grad_first, w1_ref[: 2 * LANES, :]).astype(BF16)
    grad_tail[here, :] = jnp.where(in_span, nt(grad_first, w1_tail[...]), 0.0).astype(BF16)

    @pl.when(step == pl.num_programs(0) - 1)
    def _():
        row = jnp.concatenate([place[r : r + 1, :] for r in range(place.shape[0])], axis=1)
        count = row.shape[1]
        chunk = 16
        for s in range(0, owners, chunk):
            put = jnp.where(row - s * cap == iota((chunk * cap, count), 0), 1.0, 0.0).astype(BF16)
            rows = nn(put, grad_main[...]).astype(BF16).reshape(chunk, cap, 2 * LANES)
            out_ref[s : s + chunk, :cap, :] = rows[:, :, :LANES]
            out_ref[s : s + chunk, cap : 2 * cap, :] = rows[:, :, LANES:]
        row_packed = (row // cap) * eighth + (row & (eighth - 1))
        put = jnp.where(row_packed == iota((owners * eighth, count), 0), 1.0, 0.0).astype(BF16)
        rows = nn(put, grad_tail[...]).astype(BF16)
        out_ref[:, 2 * cap :, :] = rows.reshape(owners, eighth, LANES)


def columns_kernel(cap, ids_ref, got_ref, out_ref, main):
    sources = got_ref.shape[0]
    slots = sources * cap
    eighth = cap // PACK
    quarters, _, _ = out_ref.shape
    quarter = out_ref.shape[1] * PACK // (2 * PACK + 1)
    main[:, :LANES] = got_ref[:, :cap, :].reshape(slots, LANES)
    main[:, LANES : 2 * LANES] = got_ref[:, cap : 2 * cap, :].reshape(slots, LANES)
    packed = got_ref[:, 2 * cap :, :].astype(F32)
    tail = jnp.concatenate(
        [packed] + [pltpu.roll(packed, LANES - g * SPAN, 2) for g in range(1, PACK)], axis=1
    )
    main[:, 2 * LANES :] = tail.reshape(slots, LANES).astype(BF16)
    ids = ids_ref[...]
    row = jnp.concatenate([ids[r : r + 1, :] for r in range(ids.shape[0])], axis=1)
    part = quarter // PACK
    for q in range(quarters):
        put = jnp.where(row - q * quarter == iota((quarter, slots), 0), 1.0, 0.0).astype(BF16)
        total = nn(put, main[...])
        out_ref[q, :quarter, :] = total[:, :LANES].astype(BF16)
        out_ref[q, quarter : 2 * quarter, :] = total[:, LANES : 2 * LANES].astype(BF16)
        tail = total[:, 2 * LANES :]
        lane = iota((part, LANES), 1) // SPAN
        packed = tail[:part, :]
        for g in range(1, PACK):
            packed = jnp.where(
                lane == g, pltpu.roll(tail[g * part : (g + 1) * part, :], g * SPAN, 1), packed
            )
        out_ref[q, 2 * quarter :, :] = packed.astype(BF16)


def total_kernel(parts_ref, out_ref):
    quarter, width = out_ref.shape
    part = quarter // PACK
    total = parts_ref[0].astype(F32)
    for k in range(1, parts_ref.shape[0]):
        total = total + parts_ref[k].astype(F32)
    out_ref[:, :LANES] = total[:quarter]
    out_ref[:, LANES : 2 * LANES] = total[quarter : 2 * quarter]
    packed = total[2 * quarter :]
    for g in range(PACK):
        tail = packed if g == 0 else pltpu.roll(packed, LANES - g * SPAN, 1)
        out_ref[g * part : (g + 1) * part, 2 * LANES :] = tail[:, : width - 2 * LANES]


def on_device(
    profiles, owner_block, column_offset, observed, sigma, qc_flags, w_first, w_second, w_third
):
    owners = lax.axis_size("grid")
    groups = lax.axis_size("chan")
    rows = owner_block.shape[0]
    cap = 2 * rows // owners
    cols, width = profiles.shape
    hidden, channels = w_third.shape
    quarter = cols // groups
    tiles = rows // LANES
    eighth = cap // PACK
    sds = jax.ShapeDtypeStruct

    def across(x, axis):
        return lax.all_to_all(x, axis, split_axis=0, concat_axis=0, tiled=True)

    place, request = call(
        functools.partial(slots_kernel, owners, cap),
        (sds((tiles, LANES), jnp.int32), sds((owners, cap), jnp.int32)),
        (owner_block.reshape(tiles, LANES), column_offset.reshape(tiles, LANES)),
    )
    wanted = across(request, "grid")
    bundle = sds((owners, 2 * cap + eighth, LANES), BF16)
    rows_out = call(
        functools.partial(gather_kernel, cap),
        bundle,
        (wanted, profiles),
        scratch_shapes=[pltpu.VMEM((cols, 3 * LANES), BF16)],
    )
    ids = wanted.reshape(owners * cap // LANES, LANES)
    arrived = across(rows_out, "grid")
    block = 256
    whole = lambda *shape: pl.BlockSpec(shape, lambda i: (0,) * len(shape))
    grads = call(
        functools.partial(network_kernel, cap),
        bundle,
        (place, arrived, observed, qc_flags, sigma.reshape(1, channels), w_first, w_second, w_third),
        grid=(rows // block,),
        in_specs=[
            whole(tiles, LANES),
            whole(*bundle.shape),
            pl.BlockSpec((block, channels), lambda i: (i, 0)),
            pl.BlockSpec((block, channels), lambda i: (i, 0)),
            whole(1, channels),
            whole(width, hidden),
            whole(hidden, hidden),
            whole(hidden, channels),
        ],
        out_specs=whole(*bundle.shape),
        scratch_shapes=[
            pltpu.VMEM((owners * cap, 2 * LANES), BF16),
            pltpu.VMEM((LANES, hidden), BF16),
            pltpu.VMEM((rows, 2 * LANES), BF16),
            pltpu.VMEM((rows, LANES), BF16),
        ],
    )
    got = across(grads, "grid")
    parts = call(
        functools.partial(columns_kernel, cap),
        sds((groups, 2 * quarter + quarter // PACK, LANES), BF16),
        (ids, got),
        scratch_shapes=[pltpu.VMEM((owners * cap, 3 * LANES), BF16)],
    )
    shares = across(parts, "chan")
    return call(total_kernel, sds((quarter, width), F32), (shares,))


def solution(mesh):
    in_specs = (
        P("grid", None),
        P(("grid", "chan"), None),
        P(("grid", "chan")),
        P(("grid", "chan"), None),
        P(),
        P(("grid", "chan"), None),
        P(),
        P(),
        P(),
    )
    out_specs = P(("grid", "chan"), None)
    return jax.shard_map(
        on_device, mesh=mesh, in_specs=in_specs, out_specs=out_specs, check_vma=False
    )
```

```python
import functools

import jax
import jax.numpy as jnp
from jax import lax
from jax.experimental import pallas as pl
from jax.experimental.pallas import tpu as pltpu
from jax.sharding import PartitionSpec as P

LANES = 128
PACK = 4
SPAN = LANES // PACK
F32 = jnp.float32
BF16 = jnp.bfloat16
NT = (((1,), (1,)), ((), ()))


def iota(shape, axis):
    return lax.broadcasted_iota(jnp.int32, shape, axis)


def nn(a, b):
    return jnp.dot(a, b, preferred_element_type=F32)


def nt(a, b):
    return lax.dot_general(a, b, NT, preferred_element_type=F32)


def call(kernel, out, args, vmem=48, **kw):
    return pl.pallas_call(
        kernel,
        out_shape=out,
        compiler_params=pltpu.CompilerParams(vmem_limit_bytes=vmem * 2**20),
        **kw,
    )(*args)


def slots_kernel(
    owners, cap, target_hbm, offset_hbm, place_ref, request_ref, target_ref, offset_ref, sems
):
    tiles = target_ref.shape[0]
    get_target = pltpu.make_async_copy(target_hbm, target_ref, sems.at[0])
    get_offset = pltpu.make_async_copy(offset_hbm, offset_ref, sems.at[1])
    get_target.start()
    get_offset.start()
    get_target.wait()
    get_offset.wait()
    target = target_ref[...]
    offset = offset_ref[...]
    hot = jnp.concatenate(
        [
            jnp.where(iota((owners, LANES), 0) == target[r : r + 1, :], 1.0, 0.0)
            for r in range(tiles)
        ],
        axis=1,
    )
    upper = jnp.where(iota((256, 256), 0) <= iota((256, 256), 1), 1.0, 0.0).astype(BF16)
    carry = jnp.zeros((owners, 1), F32)
    slots = []
    for b in range(tiles * LANES // 256):
        part = hot[:, b * 256 : (b + 1) * 256]
        count = nn(part.astype(BF16), upper) + carry
        carry = count[:, 255:256]
        slots.append(jnp.sum(part * (count - 1.0), axis=0, keepdims=True))
    slot = jnp.concatenate(slots, axis=1)
    high = offset // 32
    low = offset - high * 32
    flat = lambda a: jnp.concatenate([a[r : r + 1, :] for r in range(tiles)], axis=1)
    at_slot = jnp.where(
        iota((cap, tiles * LANES), 0).astype(F32) == slot, 1.0, 0.0
    )
    hot = hot.astype(BF16)
    table_high = nt(hot, (at_slot * flat(high.astype(F32))).astype(BF16))
    table_low = nt(hot, (at_slot * flat(low.astype(F32))).astype(BF16))
    filled = nt(hot, at_slot.astype(BF16))
    request_ref[...] = jnp.where(
        filled > 0.5, table_high * 32.0 + table_low, -1.0
    ).astype(jnp.int32)
    slot8 = jnp.concatenate(
        [slot[:, r * LANES : (r + 1) * LANES] for r in range(tiles)], axis=0
    )
    place_ref[...] = target * cap + slot8.astype(jnp.int32)


def gather_kernel(cap, wanted_ref, table_ref, out_ref):
    cols = table_ref.shape[0]
    sources = wanted_ref.shape[0]
    wanted = wanted_ref[...].astype(F32).T
    group = 16
    column = iota((cap, cols), 1).astype(F32)
    eighth = cap // PACK
    for s in range(0, sources, group):
        pick = jnp.concatenate(
            [
                jnp.where(wanted[:, s + j : s + j + 1] == column, 1.0, 0.0).astype(BF16)
                for j in range(group)
            ],
            axis=0,
        )
        rows = nn(pick, table_ref[...]).reshape(group, cap, 3 * LANES)
        tail = rows[:, :, 2 * LANES :]
        packed = tail[:, :eighth, :]
        for g in range(1, PACK):
            packed = packed + pltpu.roll(
                tail[:, g * eighth : (g + 1) * eighth, :], g * SPAN, 2
            )
        out_ref[s : s + group, :cap, :] = rows[:, :, :LANES].astype(BF16)
        out_ref[s : s + group, cap : 2 * cap, :] = rows[:, :, LANES : 2 * LANES].astype(BF16)
        out_ref[s : s + group, 2 * cap :, :] = packed.astype(BF16)


def network_kernel(
    cap,
    blocks,
    place_ref,
    arrived_ref,
    sigma_ref,
    observed_hbm,
    flags_hbm,
    w1_hbm,
    w2_hbm,
    w3_hbm,
    out_ref,
    observed_ref,
    flags_ref,
    w1_ref,
    w2_ref,
    w3_ref,
    main,
    w1_tail,
    grad_main,
    grad_tail,
    sems,
):
    pairs = (
        (w1_hbm, w1_ref),
        (w2_hbm, w2_ref),
        (w3_hbm, w3_ref),
        (observed_hbm, observed_ref),
        (flags_hbm, flags_ref),
    )
    get_w1, get_w2, get_w3, get_observed, get_flags = [
        pltpu.make_async_copy(src, dst, sems.at[k]) for k, (src, dst) in enumerate(pairs)
    ]
    for get in (get_w1, get_w2, get_w3, get_observed, get_flags):
        get.start()
    owners = arrived_ref.shape[0]
    slots = owners * cap
    eighth = cap // PACK
    width, hidden = w1_ref.shape
    rest = width - 2 * LANES
    count = observed_ref.shape[0]
    block = count // blocks
    tiles = block // LANES

    main[:, :LANES] = arrived_ref[:, :cap, :].reshape(slots, LANES)
    main[:, LANES:] = arrived_ref[:, cap : 2 * cap, :].reshape(slots, LANES)
    place = place_ref[...]
    packed = arrived_ref[:, 2 * cap :, :].reshape(owners * eighth, LANES)
    inverse = 1.0 / sigma_ref[...]
    each = range(blocks)
    part = [slice(b * block, (b + 1) * block) for b in each]

    in_span, inputs, inputs_tail = [], [], []
    for b in each:
        column = jnp.concatenate(
            [
                jnp.broadcast_to(place[r : r + 1, :], (LANES, LANES)).astype(F32).T
                for r in range(b * tiles, (b + 1) * tiles)
            ],
            axis=0,
        ).astype(jnp.int32)[:, :1]
        slot = column & (cap - 1)
        pick = jnp.where(column == iota((block, slots), 1), 1.0, 0.0).astype(BF16)
        packed_at = (column // cap) * eighth + (slot & (eighth - 1))
        pick_tail = jnp.where(
            packed_at == iota((block, owners * eighth), 1), 1.0, 0.0
        ).astype(BF16)
        in_span.append(iota((block, LANES), 1) // SPAN == slot // eighth)
        inputs.append(nn(pick, main[...]).astype(BF16))
        inputs_tail.append(jnp.where(in_span[b], nn(pick_tail, packed), 0.0).astype(BF16))

    get_w1.wait()
    tail = jnp.concatenate(
        [w1_ref[2 * LANES :, :].astype(F32), jnp.zeros((SPAN - rest, hidden), F32)], axis=0
    )
    w1_tail[...] = jnp.concatenate([tail] * PACK, axis=0).astype(BF16)
    first = [
        jnp.tanh(nn(inputs[b], w1_ref[: 2 * LANES, :]) + nn(inputs_tail[b], w1_tail[...])).astype(BF16)
        for b in each
    ]
    get_w2.wait()
    second = [jnp.tanh(nn(first[b], w2_ref[...])).astype(BF16) for b in each]
    get_w3.wait()
    get_observed.wait()
    get_flags.wait()
    grad_sim = []
    for b in each:
        departure = (nn(second[b], w3_ref[...]) - observed_ref[part[b], :]) * inverse
        weighted = flags_ref[part[b], :].astype(F32) * jnp.clip(departure, -1.5, 1.5)
        grad_sim.append((weighted * inverse).astype(BF16))
    grad_second, grad_first = [], []
    for b in each:
        second_f = second[b].astype(F32)
        grad_second.append(
            (nt(grad_sim[b], w3_ref[...]) * (1.0 - second_f * second_f)).astype(BF16)
        )
    for b in each:
        first_f = first[b].astype(F32)
        grad_first.append(
            (nt(grad_second[b], w2_ref[...]) * (1.0 - first_f * first_f)).astype(BF16)
        )
    for b in each:
        grad_main[part[b], :] = nt(grad_first[b], w1_ref[: 2 * LANES, :]).astype(BF16)
        grad_tail[part[b], :] = jnp.where(
            in_span[b], nt(grad_first[b], w1_tail[...]), 0.0
        ).astype(BF16)

    row = jnp.concatenate([place[r : r + 1, :] for r in range(place.shape[0])], axis=1)
    chunk = 16
    for s in range(0, owners, chunk):
        put = jnp.where(row - s * cap == iota((chunk * cap, count), 0), 1.0, 0.0).astype(BF16)
        rows = nn(put, grad_main[...]).astype(BF16).reshape(chunk, cap, 2 * LANES)
        out_ref[s : s + chunk, :cap, :] = rows[:, :, :LANES]
        out_ref[s : s + chunk, cap : 2 * cap, :] = rows[:, :, LANES:]
    row_packed = (row // cap) * eighth + (row & (eighth - 1))
    put = jnp.where(row_packed == iota((owners * eighth, count), 0), 1.0, 0.0).astype(BF16)
    rows = nn(put, grad_tail[...]).astype(BF16)
    out_ref[:, 2 * cap :, :] = rows.reshape(owners, eighth, LANES)


def open_rows(cap, got_ref, main):
    slots = got_ref.shape[0] * cap
    main[:, :LANES] = got_ref[:, :cap, :].reshape(slots, LANES)
    main[:, LANES : 2 * LANES] = got_ref[:, cap : 2 * cap, :].reshape(slots, LANES)
    packed = got_ref[:, 2 * cap :, :].astype(F32)
    tail = jnp.concatenate(
        [packed] + [pltpu.roll(packed, LANES - g * SPAN, 2) for g in range(1, PACK)], axis=1
    )
    main[:, 2 * LANES :] = tail.reshape(slots, LANES).astype(BF16)


def quarter_sums(shift, groups, quarter, ids_ref, main):
    which = lax.rem(lax.axis_index("chan") + shift, groups)
    ids = ids_ref[...] - which * quarter
    row = jnp.concatenate([ids[r : r + 1, :] for r in range(ids.shape[0])], axis=1)
    put = jnp.where(row == iota((quarter, row.shape[1]), 0), 1.0, 0.0).astype(BF16)
    return nn(put, main[...])


def others_kernel(cap, groups, quarter, ids_ref, got_ref, *refs):
    outs, main = refs[:-1], refs[-1]
    open_rows(cap, got_ref, main)
    part = quarter // PACK
    lane = iota((part, LANES), 1) // SPAN
    for k, out_ref in enumerate(outs):
        total = quarter_sums(k + 1, groups, quarter, ids_ref, main)
        out_ref[:quarter, :] = total[:, :LANES].astype(BF16)
        out_ref[quarter : 2 * quarter, :] = total[:, LANES : 2 * LANES].astype(BF16)
        tail = total[:, 2 * LANES :]
        packed = tail[:part, :]
        for g in range(1, PACK):
            packed = jnp.where(
                lane == g, pltpu.roll(tail[g * part : (g + 1) * part, :], g * SPAN, 1), packed
            )
        out_ref[2 * quarter :, :] = packed.astype(BF16)


def own_kernel(cap, groups, quarter, ids_ref, got_ref, out_ref, main):
    open_rows(cap, got_ref, main)
    out_ref[...] = quarter_sums(0, groups, quarter, ids_ref, main)


def total_kernel(own_ref, *refs):
    parts, out_ref = refs[:-1], refs[-1]
    width, quarter = out_ref.shape
    part = quarter // PACK
    total = parts[0][...].astype(F32)
    for other in parts[1:]:
        total = total + other[...].astype(F32)
    packed = total[2 * quarter :]
    tail = jnp.concatenate(
        [packed] + [pltpu.roll(packed, LANES - g * SPAN, 1) for g in range(1, PACK)], axis=0
    )
    out_ref[:LANES, :] = (own_ref[:, :LANES] + total[:quarter]).T
    out_ref[LANES : 2 * LANES, :] = (own_ref[:, LANES : 2 * LANES] + total[quarter : 2 * quarter]).T
    out_ref[2 * LANES :, :] = (own_ref[:, 2 * LANES :] + tail).T[: width - 2 * LANES, :]


def on_device(
    profiles, owner_block, column_offset, observed, sigma, qc_flags, w_first, w_second, w_third
):
    owners = lax.axis_size("grid")
    groups = lax.axis_size("chan")
    rows = owner_block.shape[0]
    cap = 2 * rows // owners
    cols, width = profiles.shape
    hidden, channels = w_third.shape
    quarter = cols // groups
    tiles = rows // LANES
    eighth = cap // PACK
    sds = jax.ShapeDtypeStruct
    local = pl.BlockSpec(memory_space=pltpu.VMEM)
    far = pl.BlockSpec(memory_space=pltpu.HBM)

    def across(x):
        return lax.all_to_all(x, "grid", split_axis=0, concat_axis=0, tiled=True)

    place, request = call(
        functools.partial(slots_kernel, owners, cap),
        (sds((tiles, LANES), jnp.int32), sds((owners, cap), jnp.int32)),
        (owner_block.reshape(tiles, LANES), column_offset.reshape(tiles, LANES)),
        in_specs=[far] * 2,
        vmem=62,
        scratch_shapes=[pltpu.VMEM((tiles, LANES), jnp.int32)] * 2
        + [pltpu.SemaphoreType.DMA((2,))],
    )
    wanted = across(request)
    table = jnp.pad(profiles, ((0, 0), (0, 3 * LANES - width)))
    bundle = sds((owners, 2 * cap + eighth, LANES), BF16)
    rows_out = call(functools.partial(gather_kernel, cap), bundle, (wanted, table))
    ids = wanted.reshape(owners * cap // LANES, LANES)
    arrived = across(rows_out)
    grads = call(
        functools.partial(network_kernel, cap, 4),
        bundle,
        (place, arrived, sigma.reshape(1, channels), observed, qc_flags, w_first, w_second, w_third),
        in_specs=[local] * 3 + [far] * 5,
        scratch_shapes=[
            pltpu.VMEM((rows, channels), F32),
            pltpu.VMEM((rows, channels), jnp.int32),
            pltpu.VMEM((width, hidden), BF16),
            pltpu.VMEM((hidden, hidden), BF16),
            pltpu.VMEM((hidden, channels), BF16),
            pltpu.VMEM((owners * cap, 2 * LANES), BF16),
            pltpu.VMEM((LANES, hidden), BF16),
            pltpu.VMEM((rows, 2 * LANES), BF16),
            pltpu.VMEM((rows, LANES), BF16),
            pltpu.SemaphoreType.DMA((5,)),
        ],
    )
    got = across(grads)
    opened = [pltpu.VMEM((owners * cap, 3 * LANES), BF16)]
    parts = call(
        functools.partial(others_kernel, cap, groups, quarter),
        [sds((2 * quarter + quarter // PACK, LANES), BF16)] * (groups - 1),
        (ids, got),
        scratch_shapes=opened,
    )
    shares = [
        lax.ppermute(part, "chan", [(i, (i + k) % groups) for i in range(groups)])
        for k, part in enumerate(parts, 1)
    ]
    own = call(
        functools.partial(own_kernel, cap, groups, quarter),
        sds((quarter, 3 * LANES), F32),
        (ids, got),
        scratch_shapes=opened,
        cost_estimate=pl.CostEstimate(flops=10**9, bytes_accessed=2 * 10**6, transcendentals=0),
    )
    return call(total_kernel, sds((width, quarter), F32), (own, *shares)).T


def solution(mesh):
    in_specs = (
        P("grid", None),
        P(("grid", "chan"), None),
        P(("grid", "chan")),
        P(("grid", "chan"), None),
        P(),
        P(("grid", "chan"), None),
        P(),
        P(),
        P(),
    )
    out_specs = P(("grid", "chan"), None)
    return jax.shard_map(
        on_device, mesh=mesh, in_specs=in_specs, out_specs=out_specs, check_vma=False
    )
```

```python
import functools

import jax
import jax.numpy as jnp
from jax import lax
from jax.experimental import pallas as pl
from jax.experimental.pallas import tpu as pltpu
from jax.sharding import PartitionSpec as P

LANES = 128
BASE = 32
F32 = jnp.float32
BF16 = jnp.bfloat16
NT = (((1,), (1,)), ((), ()))


def iota(shape, axis):
    return lax.broadcasted_iota(jnp.int32, shape, axis)


def nn(a, b):
    return jnp.dot(a, b, preferred_element_type=F32)


def nt(a, b):
    return lax.dot_general(a, b, NT, preferred_element_type=F32)


def call(kernel, out, args, vmem=48, **kw):
    return pl.pallas_call(
        kernel,
        out_shape=out,
        compiler_params=pltpu.CompilerParams(vmem_limit_bytes=vmem * 2**20),
        **kw,
    )(*args)


def flat(a):
    return jnp.concatenate([a[r : r + 1, :] for r in range(a.shape[0])], axis=1)


def push_kernel(
    owners,
    cap,
    chunk,
    target_hbm,
    offset_hbm,
    observed_hbm,
    flags_hbm,
    out_hbm,
    target_ref,
    offset_ref,
    observed_ref,
    flags_ref,
    data,
    staged,
    sems,
    out_sems,
):
    pairs = (
        (target_hbm, target_ref),
        (offset_hbm, offset_ref),
        (observed_hbm, observed_ref),
        (flags_hbm, flags_ref),
    )
    gets = [pltpu.make_async_copy(src, dst, sems.at[k]) for k, (src, dst) in enumerate(pairs)]
    for get in gets:
        get.start()
    gets[0].wait()
    gets[1].wait()
    tiles = target_ref.shape[0]
    count = tiles * LANES
    channels = observed_ref.shape[1]
    target = flat(target_ref[...])
    offset = flat(offset_ref[...])
    hot = jnp.where(iota((owners, count), 0) == target, 1.0, 0.0)
    upper = jnp.where(iota((256, 256), 0) <= iota((256, 256), 1), 1.0, 0.0).astype(BF16)
    carry = jnp.zeros((owners, 1), F32)
    slots = []
    for b in range(count // 256):
        part = hot[:, b * 256 : (b + 1) * 256]
        seen = nn(part.astype(BF16), upper) + carry
        carry = seen[:, 255:256]
        slots.append(jnp.sum(part * (seen - 1.0), axis=0, keepdims=True))
    slot = jnp.concatenate(slots, axis=1)
    place = target * cap + slot.astype(jnp.int32)
    high = offset // BASE
    low = offset - high * BASE
    at_slot = jnp.where((iota((LANES, count), 0) & (cap - 1)).astype(F32) == slot, 1.0, 0.0)
    hot = hot.astype(BF16)
    filled = nt(hot, at_slot.astype(BF16))
    high = jnp.where(filled > 0.5, nt(hot, (at_slot * high.astype(F32)).astype(BF16)), -1.0)
    low = nt(hot, (at_slot * low.astype(F32)).astype(BF16))

    gets[2].wait()
    data[:, :channels] = observed_ref[...].astype(BF16)
    gets[3].wait()
    data[:, channels:] = flags_ref[...].astype(F32).astype(BF16)
    parts = 2 * channels // LANES
    puts = []
    for k, s in enumerate(range(0, owners, chunk)):
        put = jnp.where(place - s * cap == iota((chunk * cap, count), 0), 1.0, 0.0).astype(BF16)
        rows = nn(put, data[...]).astype(BF16).reshape(chunk, cap, 2 * channels)
        for j in range(parts):
            staged[s : s + chunk, j * cap : (j + 1) * cap, :] = rows[:, :, j * LANES : (j + 1) * LANES]
        digits = jnp.where(
            iota((chunk, 8, LANES), 1) == 0,
            high[s : s + chunk, :].reshape(chunk, 1, LANES),
            low[s : s + chunk, :].reshape(chunk, 1, LANES),
        )
        staged[s : s + chunk, parts * cap :, :] = digits.astype(BF16)
        puts.append(
            pltpu.make_async_copy(
                staged.at[pl.ds(s, chunk)], out_hbm.at[pl.ds(s, chunk)], out_sems.at[k]
            )
        )
        puts[-1].start()
    for put in puts:
        put.wait()


def forward_kernel(quarter, table_ref, w1_ref, w2_ref, w3_ref, evolved_ref, first_ref, second_ref):
    first = jnp.tanh(nn(table_ref[...], w1_ref[...])).astype(BF16)
    second = jnp.tanh(nn(first, w2_ref[...])).astype(BF16)
    evolved_ref[...] = nn(second, w3_ref[...]).astype(BF16)
    mine = pl.ds(pl.multiple_of(lax.axis_index("chan") * quarter, quarter), quarter)
    first = jnp.tanh(nn(table_ref[mine, :], w1_ref[...])).astype(BF16)
    first_ref[...] = first
    second_ref[...] = jnp.tanh(nn(first, w2_ref[...])).astype(BF16)


def departures_kernel(cap, chunk, arrived_ref, evolved_ref, sigma_ref, out_ref, ids_ref):
    sources = arrived_ref.shape[0]
    cols, channels = evolved_ref.shape
    parts = channels // LANES
    digits = arrived_ref[:, 2 * parts * cap :, :].reshape(sources * 8, LANES)
    row = iota((sources, sources * 8), 1) - 8 * iota((sources, sources * 8), 0)
    high = nn(jnp.where(row == 0, 1.0, 0.0).astype(BF16), digits)
    low = nn(jnp.where(row == 1, 1.0, 0.0).astype(BF16), digits)
    per = LANES // cap
    mine = iota((sources, LANES), 1) // cap == iota((sources, LANES), 0) % per
    gather = jnp.where(
        iota((sources // per, sources), 1) // per == iota((sources // per, sources), 0), 1.0, 0.0
    ).astype(BF16)
    spread = lambda a: nn(gather, jnp.where(mine, a, 0.0).astype(BF16))
    ids_ref[...] = (spread(high) * BASE + spread(low)).astype(jnp.int32)
    column = (high * BASE + low).T
    wide = iota((cap, cols), 1).astype(F32)
    inverse = 1.0 / sigma_ref[...]
    for s in range(0, sources, chunk):
        pick = jnp.concatenate(
            [
                jnp.where(column[:cap, s + j : s + j + 1] == wide, 1.0, 0.0).astype(BF16)
                for j in range(chunk)
            ],
            axis=0,
        )
        evolved = nn(pick, evolved_ref[...])
        for j in range(parts):
            lanes = slice(j * LANES, (j + 1) * LANES)
            take = lambda k: arrived_ref[s : s + chunk, k * cap : (k + 1) * cap, :].reshape(
                chunk * cap, LANES
            ).astype(F32)
            departure = (evolved[:, lanes] - take(j)) * inverse[:, lanes]
            weighted = take(parts + j) * jnp.clip(departure, -1.5, 1.5) * inverse[:, lanes]
            out_ref[s * cap : (s + chunk) * cap, lanes] = weighted.astype(BF16)


def sums_kernel(shift, groups, ids_ref, departures_ref, out_ref):
    quarter = out_ref.shape[0]
    which = lax.rem(lax.axis_index("chan") + shift, groups)
    row = flat(ids_ref[...] - which * quarter)
    put = jnp.where(row == iota((quarter, row.shape[1]), 0), 1.0, 0.0).astype(BF16)
    out_ref[...] = nn(put, departures_ref[...]).astype(out_ref.dtype)


def adjoint_kernel(own_ref, *refs):
    parts, (first_ref, second_ref, w1_ref, w2_ref, w3_ref, out_ref) = refs[:-6], refs[-6:]
    total = own_ref[...]
    for part in parts:
        total = total + part[...].astype(F32)
    second = second_ref[...].astype(F32)
    grad_second = (nt(total.astype(BF16), w3_ref[...]) * (1.0 - second * second)).astype(BF16)
    first = first_ref[...].astype(F32)
    grad_first = (nt(grad_second, w2_ref[...]) * (1.0 - first * first)).astype(BF16)
    grads = nt(grad_first, w1_ref[...])
    width = out_ref.shape[0]
    for j in range(0, width, LANES):
        out_ref[j : min(j + LANES, width), :] = grads[:, j : j + LANES].T[: min(LANES, width - j), :]


def on_device(
    profiles, owner_block, column_offset, observed, sigma, qc_flags, w_first, w_second, w_third
):
    owners = lax.axis_size("grid")
    groups = lax.axis_size("chan")
    rows = owner_block.shape[0]
    cap = 2 * rows // owners
    cols, width = profiles.shape
    hidden, channels = w_third.shape
    quarter = cols // groups
    tiles = rows // LANES
    chunk = 16
    sds = jax.ShapeDtypeStruct
    far = pl.BlockSpec(memory_space=pltpu.HBM)

    bundle = sds((owners, 2 * channels // LANES * cap + 8, LANES), BF16)
    pushed = call(
        functools.partial(push_kernel, owners, cap, chunk),
        bundle,
        (owner_block.reshape(tiles, LANES), column_offset.reshape(tiles, LANES), observed, qc_flags),
        vmem=62,
        in_specs=[far] * 4,
        out_specs=far,
        scratch_shapes=[
            pltpu.VMEM((tiles, LANES), jnp.int32),
            pltpu.VMEM((tiles, LANES), jnp.int32),
            pltpu.VMEM((rows, channels), F32),
            pltpu.VMEM((rows, channels), jnp.int32),
            pltpu.VMEM((rows, 2 * channels), BF16),
            pltpu.VMEM(bundle.shape, BF16),
            pltpu.SemaphoreType.DMA((4,)),
            pltpu.SemaphoreType.DMA((owners // chunk,)),
        ],
    )
    arrived = lax.all_to_all(pushed, "grid", split_axis=0, concat_axis=0, tiled=True)

    padded = -(-width // LANES) * LANES
    table = jnp.pad(profiles, ((0, 0), (0, padded - width)))
    w1 = jnp.pad(w_first, ((0, padded - width), (0, 0)))
    evolved, first, second = call(
        functools.partial(forward_kernel, quarter),
        (sds((cols, channels), BF16), sds((quarter, hidden), BF16), sds((quarter, hidden), BF16)),
        (table, w1, w_second, w_third),
        cost_estimate=pl.CostEstimate(flops=2 * 10**9, bytes_accessed=4 * 10**6, transcendentals=10**6),
    )

    departures, ids = call(
        functools.partial(departures_kernel, cap, chunk),
        (sds((owners * cap, channels), BF16), sds((owners * cap // LANES, LANES), jnp.int32)),
        (arrived, evolved, sigma.reshape(1, channels)),
    )
    summed = lambda shift, dtype: call(
        functools.partial(sums_kernel, shift, groups),
        sds((quarter, channels), dtype),
        (ids, departures),
        cost_estimate=pl.CostEstimate(flops=10**9, bytes_accessed=2 * 10**6, transcendentals=0),
    )
    order = sorted(range(1, groups), key=lambda k: -min(k, groups - k))
    shares = [
        lax.ppermute(summed(k, BF16), "chan", [(i, (i + k) % groups) for i in range(groups)])
        for k in order
    ]
    return call(
        adjoint_kernel,
        sds((width, quarter), F32),
        (summed(0, F32), *shares, first, second, w1, w_second, w_third),
    ).T


def solution(mesh):
    in_specs = (
        P("grid", None),
        P(("grid", "chan"), None),
        P(("grid", "chan")),
        P(("grid", "chan"), None),
        P(),
        P(("grid", "chan"), None),
        P(),
        P(),
        P(),
    )
    out_specs = P(("grid", "chan"), None)
    return jax.shard_map(
        on_device, mesh=mesh, in_specs=in_specs, out_specs=out_specs, check_vma=False
    )
```

```python
import functools
import itertools
import math

import jax
import jax.numpy as jnp
from jax import lax
from jax.experimental import pallas as pl
from jax.experimental.pallas import tpu as pltpu
from jax.sharding import PartitionSpec as P

LANES = 128
BASE = 32
AXES = ("zhi", "zlo", "y", "core", "chan")
GROUP = AXES[1:]
GRID = AXES[:-1]


def home(zhi, core, chan, places):
    return (zhi + chan + 2 * core) % places


def devices(sizes):
    return list(itertools.product(*(range(n) for n in sizes)))
F32 = jnp.float32
BF16 = jnp.bfloat16
NT = (((1,), (1,)), ((), ()))


def iota(shape, axis):
    return lax.broadcasted_iota(jnp.int32, shape, axis)


def nn(a, b):
    return jnp.dot(a, b, preferred_element_type=F32)


def nt(a, b):
    return lax.dot_general(a, b, NT, preferred_element_type=F32)


def call(kernel, out, args, vmem=48, **kw):
    return pl.pallas_call(
        kernel,
        out_shape=out,
        compiler_params=pltpu.CompilerParams(vmem_limit_bytes=vmem * 2**20),
        **kw,
    )(*args)


def flat(a):
    return jnp.concatenate([a[r : r + 1, :] for r in range(a.shape[0])], axis=1)


def push_kernel(
    owners,
    cap,
    chunk,
    target_hbm,
    offset_hbm,
    observed_hbm,
    flags_hbm,
    out_hbm,
    target_ref,
    offset_ref,
    observed_ref,
    flags_ref,
    data,
    staged,
    sems,
    out_sems,
):
    pairs = (
        (target_hbm, target_ref),
        (offset_hbm, offset_ref),
        (observed_hbm, observed_ref),
        (flags_hbm, flags_ref),
    )
    gets = [pltpu.make_async_copy(src, dst, sems.at[k]) for k, (src, dst) in enumerate(pairs)]
    for get in gets:
        get.start()
    gets[0].wait()
    gets[1].wait()
    tiles = target_ref.shape[0]
    count = tiles * LANES
    channels = observed_ref.shape[1]
    owner = flat(target_ref[...])
    places = lax.axis_size("zhi")
    near = owners // places
    ring = (owner // near - lax.axis_index("zhi") - 2 * (owner & 1) + 2 * places) & (places - 1)
    target = (owner & (near - 1)) * places + ring
    offset = flat(offset_ref[...])
    hot = jnp.where(iota((owners, count), 0) == target, 1.0, 0.0)
    upper = jnp.where(iota((256, 256), 0) <= iota((256, 256), 1), 1.0, 0.0).astype(BF16)
    carry = jnp.zeros((owners, 1), F32)
    slots = []
    for b in range(count // 256):
        part = hot[:, b * 256 : (b + 1) * 256]
        seen = nn(part.astype(BF16), upper) + carry
        carry = seen[:, 255:256]
        slots.append(jnp.sum(part * (seen - 1.0), axis=0, keepdims=True))
    slot = jnp.concatenate(slots, axis=1)
    place = target * cap + slot.astype(jnp.int32)
    high = offset // BASE
    low = offset - high * BASE
    at_slot = jnp.where((iota((LANES, count), 0) & (cap - 1)).astype(F32) == slot, 1.0, 0.0)
    hot = hot.astype(BF16)
    filled = nt(hot, at_slot.astype(BF16))
    high = jnp.where(filled > 0.5, nt(hot, (at_slot * high.astype(F32)).astype(BF16)), -1.0)
    low = nt(hot, (at_slot * low.astype(F32)).astype(BF16))

    gets[2].wait()
    data[:, :channels] = observed_ref[...].astype(BF16)
    gets[3].wait()
    data[:, channels:] = flags_ref[...].astype(F32).astype(BF16)
    parts = 2 * channels // LANES
    puts = []
    for k, s in enumerate(range(0, owners, chunk)):
        put = jnp.where(place - s * cap == iota((chunk * cap, count), 0), 1.0, 0.0).astype(BF16)
        rows = nn(put, data[...]).astype(BF16).reshape(chunk, cap, 2 * channels)
        for j in range(parts):
            staged[s : s + chunk, j * cap : (j + 1) * cap, :] = rows[:, :, j * LANES : (j + 1) * LANES]
        digits = jnp.where(
            iota((chunk, 8, LANES), 1) == 0,
            high[s : s + chunk, :].reshape(chunk, 1, LANES),
            low[s : s + chunk, :].reshape(chunk, 1, LANES),
        )
        staged[s : s + chunk, parts * cap :, :] = digits.astype(BF16)
        puts.append(
            pltpu.make_async_copy(
                staged.at[pl.ds(s, chunk)], out_hbm.at[pl.ds(s, chunk)], out_sems.at[k]
            )
        )
        puts[-1].start()
    for put in puts:
        put.wait()


def forward_kernel(table_ref, w1_ref, w2_ref, w3_ref, evolved_ref):
    first = jnp.tanh(nn(table_ref[...], w1_ref[...])).astype(BF16)
    second = jnp.tanh(nn(first, w2_ref[...])).astype(BF16)
    evolved_ref[...] = nn(second, w3_ref[...]).astype(BF16)


def hidden_kernel(table_ref, w1_ref, w2_ref, first_ref, second_ref):
    quarter = first_ref.shape[0]
    mine = pl.ds(pl.multiple_of(lax.axis_index("chan") * quarter, quarter), quarter)
    first = jnp.tanh(nn(table_ref[mine, :], w1_ref[...])).astype(BF16)
    first_ref[...] = first
    second_ref[...] = jnp.tanh(nn(first, w2_ref[...])).astype(BF16)


def departures_kernel(cap, chunk, arrived_ref, evolved_ref, sigma_ref, out_ref, ids_ref):
    sources = arrived_ref.shape[0]
    cols, channels = evolved_ref.shape
    parts = channels // LANES
    digits = arrived_ref[:, 2 * parts * cap :, :].reshape(sources * 8, LANES)
    row = iota((sources, sources * 8), 1) - 8 * iota((sources, sources * 8), 0)
    high = nn(jnp.where(row == 0, 1.0, 0.0).astype(BF16), digits)
    low = nn(jnp.where(row == 1, 1.0, 0.0).astype(BF16), digits)
    per = LANES // cap
    mine = iota((sources, LANES), 1) // cap == iota((sources, LANES), 0) % per
    gather = jnp.where(
        iota((sources // per, sources), 1) // per == iota((sources // per, sources), 0), 1.0, 0.0
    ).astype(BF16)
    spread = lambda a: nn(gather, jnp.where(mine, a, 0.0).astype(BF16))
    ids_ref[...] = (spread(high) * BASE + spread(low)).astype(jnp.int32)
    column = (high * BASE + low).T
    wide = iota((cap, cols), 1).astype(F32)
    inverse = 1.0 / sigma_ref[...]
    for s in range(0, sources, chunk):
        pick = jnp.concatenate(
            [
                jnp.where(column[:cap, s + j : s + j + 1] == wide, 1.0, 0.0).astype(BF16)
                for j in range(chunk)
            ],
            axis=0,
        )
        evolved = nn(pick, evolved_ref[...])
        for j in range(parts):
            lanes = slice(j * LANES, (j + 1) * LANES)
            take = lambda k: arrived_ref[s : s + chunk, k * cap : (k + 1) * cap, :].reshape(
                chunk * cap, LANES
            ).astype(F32)
            departure = (evolved[:, lanes] - take(j)) * inverse[:, lanes]
            weighted = take(parts + j) * jnp.clip(departure, -1.5, 1.5) * inverse[:, lanes]
            out_ref[s * cap : (s + chunk) * cap, lanes] = weighted.astype(BF16)


def sums_kernel(shift, groups, ids_ref, departures_ref, out_ref):
    quarter = out_ref.shape[0]
    which = lax.rem(lax.axis_index("chan") + shift, groups)
    row = flat(ids_ref[...] - which * quarter)
    put = jnp.where(row == iota((quarter, row.shape[1]), 0), 1.0, 0.0).astype(BF16)
    out_ref[...] = nn(put, departures_ref[...]).astype(out_ref.dtype)


def adjoint_kernel(*refs):
    parts, (first_ref, second_ref, w1_ref, w2_ref, w3_ref, out_ref) = refs[:-6], refs[-6:]
    total = parts[0][...].astype(F32)
    for part in parts[1:]:
        total = total + part[...].astype(F32)
    second = second_ref[...].astype(F32)
    grad_second = (nt(total.astype(BF16), w3_ref[...]) * (1.0 - second * second)).astype(BF16)
    first = first_ref[...].astype(F32)
    grad_first = (nt(grad_second, w2_ref[...]) * (1.0 - first * first)).astype(BF16)
    grads = nt(grad_first, w1_ref[...])
    width = out_ref.shape[0]
    for j in range(0, width, LANES):
        out_ref[j : min(j + LANES, width), :] = grads[:, j : j + LANES].T[: min(LANES, width - j), :]


def on_device(
    profiles, owner_block, column_offset, observed, sigma, qc_flags, w_first, w_second, w_third
):
    sizes = tuple(lax.axis_size(name) for name in AXES)
    owners = math.prod(sizes[:-1])
    places, groups = sizes[0], sizes[-1]
    everyone = devices(sizes)
    number = {place: i for i, place in enumerate(everyone)}
    rows = owner_block.shape[0]
    cap = 2 * rows // owners
    cols, width = profiles.shape
    hidden, channels = w_third.shape
    quarter = cols // groups
    tiles = rows // LANES
    chunk = 16
    sds = jax.ShapeDtypeStruct
    far = pl.BlockSpec(memory_space=pltpu.HBM)

    def at_home(place, chan):
        return number[(home(place[0], place[3], place[4], places), *place[1:4], chan)]

    fetched = lax.ppermute(profiles.T, AXES, [(at_home(p, p[4]), number[p]) for p in everyone])

    bundle = sds((owners, 2 * channels // LANES * cap + 8, LANES), BF16)
    pushed = call(
        functools.partial(push_kernel, owners, cap, chunk),
        bundle,
        (owner_block.reshape(tiles, LANES), column_offset.reshape(tiles, LANES), observed, qc_flags),
        vmem=62,
        in_specs=[far] * 4,
        out_specs=far,
        scratch_shapes=[
            pltpu.VMEM((tiles, LANES), jnp.int32),
            pltpu.VMEM((tiles, LANES), jnp.int32),
            pltpu.VMEM((rows, channels), F32),
            pltpu.VMEM((rows, channels), jnp.int32),
            pltpu.VMEM((rows, 2 * channels), BF16),
            pltpu.VMEM(bundle.shape, BF16),
            pltpu.SemaphoreType.DMA((4,)),
            pltpu.SemaphoreType.DMA((owners // chunk,)),
        ],
    )
    arrived = lax.all_to_all(pushed, GROUP, split_axis=0, concat_axis=0, tiled=True)

    padded = -(-width // LANES) * LANES
    wide = lambda a, axis: jnp.pad(a, [(0, padded - width) if k == axis else (0, 0) for k in (0, 1)])
    w1 = wide(w_first, 0)
    evolved = call(
        forward_kernel,
        sds((cols, channels), BF16),
        (wide(fetched.T, 1), w1, w_second, w_third),
        vmem=24,
        cost_estimate=pl.CostEstimate(flops=10**11, bytes_accessed=4 * 10**6, transcendentals=10**6),
    )
    first, second = call(
        hidden_kernel,
        [sds((quarter, hidden), BF16)] * 2,
        (wide(profiles, 1), w1, w_second),
        vmem=24,
    )

    departures, ids = call(
        functools.partial(departures_kernel, cap, chunk),
        (sds((owners * cap, channels), BF16), sds((owners * cap // LANES, LANES), jnp.int32)),
        (arrived, evolved, sigma.reshape(1, channels)),
        vmem=32,
    )
    summed = lambda shift, dtype: call(
        functools.partial(sums_kernel, shift, groups),
        sds((quarter, channels), dtype),
        (ids, departures),
        vmem=24,
        cost_estimate=pl.CostEstimate(flops=10**9, bytes_accessed=2 * 10**6, transcendentals=0),
    )
    order = sorted(range(groups), key=lambda k: -min(k, groups - k))
    shares = [
        lax.ppermute(
            summed(k, BF16), AXES, [(number[p], at_home(p, (p[4] + k) % groups)) for p in everyone]
        )
        for k in order
    ]
    return call(
        adjoint_kernel,
        sds((width, quarter), F32),
        (*shares, first, second, w1, w_second, w_third),
        vmem=24,
    ).T


def solution(mesh):
    grid, chan = mesh.devices.shape
    places = 4
    near = jax.sharding.Mesh(mesh.devices.reshape(places, 2, grid // (4 * places), 2, chan), AXES)
    whole = P((*GRID, "chan"), None)
    in_specs = (P(GRID, None), whole, P((*GRID, "chan")), whole, P(), whole, P(), P(), P())
    return jax.shard_map(on_device, mesh=near, in_specs=in_specs, out_specs=whole, check_vma=False)
```

```python
import functools
import itertools
import math

import jax
import jax.numpy as jnp
from jax import lax
from jax.experimental import pallas as pl
from jax.experimental.pallas import tpu as pltpu
from jax.sharding import PartitionSpec as P

LANES = 128
PACK = 4
SPAN = LANES // PACK
BASE = 32
AXES = ("zhi", "zlo", "y", "core", "chan")
GROUP = AXES[1:]
GRID = AXES[:-1]


def home(zhi, core, chan, places):
    return (zhi + chan + 2 * core) % places


def devices(sizes):
    return list(itertools.product(*(range(n) for n in sizes)))
F32 = jnp.float32
BF16 = jnp.bfloat16
NT = (((1,), (1,)), ((), ()))


def iota(shape, axis):
    return lax.broadcasted_iota(jnp.int32, shape, axis)


def nn(a, b):
    return jnp.dot(a, b, preferred_element_type=F32)


def nt(a, b):
    return lax.dot_general(a, b, NT, preferred_element_type=F32)


def call(kernel, out, args, vmem=48, **kw):
    return pl.pallas_call(
        kernel,
        out_shape=out,
        compiler_params=pltpu.CompilerParams(vmem_limit_bytes=vmem * 2**20),
        **kw,
    )(*args)


def flat(a):
    return jnp.concatenate([a[r : r + 1, :] for r in range(a.shape[0])], axis=1)


def push_kernel(
    owners,
    cap,
    chunk,
    target_hbm,
    offset_hbm,
    observed_hbm,
    flags_hbm,
    out_hbm,
    target_ref,
    offset_ref,
    observed_ref,
    flags_ref,
    data,
    staged,
    sems,
    out_sems,
):
    pairs = (
        (target_hbm, target_ref),
        (offset_hbm, offset_ref),
        (observed_hbm, observed_ref),
        (flags_hbm, flags_ref),
    )
    gets = [pltpu.make_async_copy(src, dst, sems.at[k]) for k, (src, dst) in enumerate(pairs)]
    for get in gets:
        get.start()
    gets[0].wait()
    gets[1].wait()
    tiles = target_ref.shape[0]
    count = tiles * LANES
    channels = observed_ref.shape[1]
    owner = flat(target_ref[...])
    places = lax.axis_size("zhi")
    near = owners // places
    ring = (owner // near - lax.axis_index("zhi") - 2 * (owner & 1) + 2 * places) & (places - 1)
    target = (owner & (near - 1)) * places + ring
    offset = flat(offset_ref[...])
    hot = jnp.where(iota((owners, count), 0) == target, 1.0, 0.0)
    upper = jnp.where(iota((256, 256), 0) <= iota((256, 256), 1), 1.0, 0.0).astype(BF16)
    carry = jnp.zeros((owners, 1), F32)
    slots = []
    for b in range(count // 256):
        part = hot[:, b * 256 : (b + 1) * 256]
        seen = nn(part.astype(BF16), upper) + carry
        carry = seen[:, 255:256]
        slots.append(jnp.sum(part * (seen - 1.0), axis=0, keepdims=True))
    slot = jnp.concatenate(slots, axis=1)
    place = target * cap + slot.astype(jnp.int32)
    high = offset // BASE
    low = offset - high * BASE
    at_slot = jnp.where((iota((LANES, count), 0) & (cap - 1)).astype(F32) == slot, 1.0, 0.0)
    hot = hot.astype(BF16)
    filled = nt(hot, at_slot.astype(BF16))
    high = jnp.where(filled > 0.5, nt(hot, (at_slot * high.astype(F32)).astype(BF16)), -1.0)
    low = nt(hot, (at_slot * low.astype(F32)).astype(BF16))

    gets[2].wait()
    data[:, :channels] = observed_ref[...].astype(BF16)
    gets[3].wait()
    data[:, channels:] = flags_ref[...].astype(F32).astype(BF16)
    parts = 2 * channels // LANES
    puts = []
    for k, s in enumerate(range(0, owners, chunk)):
        put = jnp.where(place - s * cap == iota((chunk * cap, count), 0), 1.0, 0.0).astype(BF16)
        rows = nn(put, data[...]).astype(BF16).reshape(chunk, cap, 2 * channels)
        for j in range(parts):
            staged[s : s + chunk, j * cap : (j + 1) * cap, :] = rows[:, :, j * LANES : (j + 1) * LANES]
        digits = jnp.where(
            iota((chunk, 8, LANES), 1) == 0,
            high[s : s + chunk, :].reshape(chunk, 1, LANES),
            low[s : s + chunk, :].reshape(chunk, 1, LANES),
        )
        staged[s : s + chunk, parts * cap :, :] = digits.astype(BF16)
        puts.append(
            pltpu.make_async_copy(
                staged.at[pl.ds(s, chunk)], out_hbm.at[pl.ds(s, chunk)], out_sems.at[k]
            )
        )
        puts[-1].start()
    for put in puts:
        put.wait()


def forward_kernel(table_ref, w1_ref, w2_ref, w3_ref, evolved_ref, first_ref, second_ref):
    first = jnp.tanh(nn(table_ref[...], w1_ref[...])).astype(BF16)
    second = jnp.tanh(nn(first, w2_ref[...])).astype(BF16)
    first_ref[...] = first
    second_ref[...] = second
    evolved_ref[...] = nn(second, w3_ref[...]).astype(BF16)


def departures_kernel(cap, chunk, arrived_ref, evolved_ref, sigma_ref, out_ref, ids_ref):
    sources = arrived_ref.shape[0]
    cols, channels = evolved_ref.shape
    parts = channels // LANES
    digits = arrived_ref[:, 2 * parts * cap :, :].reshape(sources * 8, LANES)
    row = iota((sources, sources * 8), 1) - 8 * iota((sources, sources * 8), 0)
    high = nn(jnp.where(row == 0, 1.0, 0.0).astype(BF16), digits)
    low = nn(jnp.where(row == 1, 1.0, 0.0).astype(BF16), digits)
    per = LANES // cap
    mine = iota((sources, LANES), 1) // cap == iota((sources, LANES), 0) % per
    gather = jnp.where(
        iota((sources // per, sources), 1) // per == iota((sources // per, sources), 0), 1.0, 0.0
    ).astype(BF16)
    spread = lambda a: nn(gather, jnp.where(mine, a, 0.0).astype(BF16))
    ids_ref[...] = (spread(high) * BASE + spread(low)).astype(jnp.int32)
    column = (high * BASE + low).T
    wide = iota((cap, cols), 1).astype(F32)
    inverse = 1.0 / sigma_ref[...]
    for s in range(0, sources, chunk):
        pick = jnp.concatenate(
            [
                jnp.where(column[:cap, s + j : s + j + 1] == wide, 1.0, 0.0).astype(BF16)
                for j in range(chunk)
            ],
            axis=0,
        )
        evolved = nn(pick, evolved_ref[...])
        for j in range(parts):
            lanes = slice(j * LANES, (j + 1) * LANES)
            take = lambda k: arrived_ref[s : s + chunk, k * cap : (k + 1) * cap, :].reshape(
                chunk * cap, LANES
            ).astype(F32)
            departure = (evolved[:, lanes] - take(j)) * inverse[:, lanes]
            weighted = take(parts + j) * jnp.clip(departure, -1.5, 1.5) * inverse[:, lanes]
            out_ref[s * cap : (s + chunk) * cap, lanes] = weighted.astype(BF16)


def adjoint_kernel(
    shift, groups, quarter, ids_ref, departures_ref, first_ref, second_ref, w1_ref, w2_ref, w3_ref, out_ref
):
    which = lax.rem(lax.axis_index("chan") + shift, groups)
    row = flat(ids_ref[...] - which * quarter)
    put = jnp.where(row == iota((quarter, row.shape[1]), 0), 1.0, 0.0).astype(BF16)
    total = nn(put, departures_ref[...]).astype(BF16)
    mine = pl.ds(pl.multiple_of(which * quarter, quarter), quarter)
    second = second_ref[mine, :].astype(F32)
    grad_second = (nt(total, w3_ref[...]) * (1.0 - second * second)).astype(BF16)
    first = first_ref[mine, :].astype(F32)
    grad_first = (nt(grad_second, w2_ref[...]) * (1.0 - first * first)).astype(BF16)
    grads = nt(grad_first, w1_ref[...])
    part = quarter // PACK
    lane = iota((part, LANES), 1) // SPAN
    out_ref[:quarter, :] = grads[:, :LANES].astype(BF16)
    out_ref[quarter : 2 * quarter, :] = grads[:, LANES : 2 * LANES].astype(BF16)
    tail = grads[:, 2 * LANES :]
    packed = tail[:part, :]
    for g in range(1, PACK):
        packed = jnp.where(
            lane == g, pltpu.roll(tail[g * part : (g + 1) * part, :], g * SPAN, 1), packed
        )
    out_ref[2 * quarter :, :] = packed.astype(BF16)


def add_kernel(so_far_ref, part_ref, out_ref):
    out_ref[...] = so_far_ref[...].astype(F32) + part_ref[...].astype(F32)


def total_kernel(so_far_ref, part_ref, out_ref):
    width, quarter = out_ref.shape
    total = so_far_ref[...] + part_ref[...].astype(F32)
    packed = total[2 * quarter :]
    tail = jnp.concatenate(
        [packed] + [pltpu.roll(packed, LANES - g * SPAN, 1) for g in range(1, PACK)], axis=0
    )
    out_ref[:LANES, :] = total[:quarter].T
    out_ref[LANES : 2 * LANES, :] = total[quarter : 2 * quarter].T
    out_ref[2 * LANES :, :] = tail.T[: width - 2 * LANES, :]


def on_device(
    profiles, owner_block, column_offset, observed, sigma, qc_flags, w_first, w_second, w_third
):
    sizes = tuple(lax.axis_size(name) for name in AXES)
    owners = math.prod(sizes[:-1])
    places, groups = sizes[0], sizes[-1]
    everyone = devices(sizes)
    number = {place: i for i, place in enumerate(everyone)}
    rows = owner_block.shape[0]
    cap = 2 * rows // owners
    cols, width = profiles.shape
    hidden, channels = w_third.shape
    quarter = cols // groups
    tiles = rows // LANES
    chunk = 16
    sds = jax.ShapeDtypeStruct
    far = pl.BlockSpec(memory_space=pltpu.HBM)

    def at_home(place, chan):
        return number[(home(place[0], place[3], place[4], places), *place[1:4], chan)]

    fetched = lax.ppermute(profiles.T, AXES, [(at_home(p, p[4]), number[p]) for p in everyone])

    bundle = sds((owners, 2 * channels // LANES * cap + 8, LANES), BF16)
    pushed = call(
        functools.partial(push_kernel, owners, cap, chunk),
        bundle,
        (owner_block.reshape(tiles, LANES), column_offset.reshape(tiles, LANES), observed, qc_flags),
        vmem=62,
        in_specs=[far] * 4,
        out_specs=far,
        scratch_shapes=[
            pltpu.VMEM((tiles, LANES), jnp.int32),
            pltpu.VMEM((tiles, LANES), jnp.int32),
            pltpu.VMEM((rows, channels), F32),
            pltpu.VMEM((rows, channels), jnp.int32),
            pltpu.VMEM((rows, 2 * channels), BF16),
            pltpu.VMEM(bundle.shape, BF16),
            pltpu.SemaphoreType.DMA((4,)),
            pltpu.SemaphoreType.DMA((owners // chunk,)),
        ],
    )
    arrived = lax.all_to_all(pushed, GROUP, split_axis=0, concat_axis=0, tiled=True)

    padded = -(-width // LANES) * LANES
    wide = lambda a, axis: jnp.pad(a, [(0, padded - width) if k == axis else (0, 0) for k in (0, 1)])
    w1 = wide(w_first, 0)
    evolved, first, second = call(
        forward_kernel,
        (sds((cols, channels), BF16), sds((cols, hidden), BF16), sds((cols, hidden), BF16)),
        (wide(fetched.T, 1), w1, w_second, w_third),
        vmem=24,
        cost_estimate=pl.CostEstimate(flops=10**11, bytes_accessed=4 * 10**6, transcendentals=10**6),
    )

    departures, ids = call(
        functools.partial(departures_kernel, cap, chunk),
        (sds((owners * cap, channels), BF16), sds((owners * cap // LANES, LANES), jnp.int32)),
        (arrived, evolved, sigma.reshape(1, channels)),
        vmem=32,
    )
    def gradients(shift):
        return call(
            functools.partial(adjoint_kernel, shift, groups, quarter),
            sds((2 * quarter + quarter // PACK, LANES), BF16),
            (ids, departures, first, second, w1, w_second, w_third),
            vmem=24,
            cost_estimate=pl.CostEstimate(flops=2 * 10**9, bytes_accessed=10**6, transcendentals=0),
        )

    order = sorted(range(groups), key=lambda k: -min(k, groups - k))
    shares = [
        lax.ppermute(
            gradients(k), AXES, [(number[p], at_home(p, (p[4] + k) % groups)) for p in everyone]
        )
        for k in order
    ]
    total = shares[0]
    for share in shares[1:-1]:
        total = call(
            add_kernel,
            sds(share.shape, F32),
            (total, share),
            vmem=24,
            cost_estimate=pl.CostEstimate(flops=10**10, bytes_accessed=10**6, transcendentals=0),
        )
    return call(total_kernel, sds((width, quarter), F32), (total, shares[-1]), vmem=24).T


def solution(mesh):
    grid, chan = mesh.devices.shape
    places = 4
    near = jax.sharding.Mesh(mesh.devices.reshape(places, 2, grid // (4 * places), 2, chan), AXES)
    whole = P((*GRID, "chan"), None)
    in_specs = (P(GRID, None), whole, P((*GRID, "chan")), whole, P(), whole, P(), P(), P())
    return jax.shard_map(on_device, mesh=near, in_specs=in_specs, out_specs=whole, check_vma=False)
```

```python
import functools
import itertools
import math

import jax
import jax.numpy as jnp
from jax import lax
from jax.experimental import pallas as pl
from jax.experimental.pallas import tpu as pltpu
from jax.sharding import PartitionSpec as P

LANES = 128
PACK = 4
SPAN = LANES // PACK
BASE = 32
AXES = ("zhi", "zlo", "y", "core", "chan")
GROUP = AXES[1:]
GRID = AXES[:-1]


def home(place, places):
    zhi, zlo, y, core, chan = place
    shift = (chan + 2 * core) % places
    return (zhi + shift) % places, zlo ^ int(shift == places // 2), y, core


def devices(sizes):
    return list(itertools.product(*(range(n) for n in sizes)))
F32 = jnp.float32
BF16 = jnp.bfloat16
NT = (((1,), (1,)), ((), ()))


def iota(shape, axis):
    return lax.broadcasted_iota(jnp.int32, shape, axis)


def nn(a, b):
    return jnp.dot(a, b, preferred_element_type=F32)


def nt(a, b):
    return lax.dot_general(a, b, NT, preferred_element_type=F32)


def call(kernel, out, args, vmem=48, **kw):
    return pl.pallas_call(
        kernel,
        out_shape=out,
        compiler_params=pltpu.CompilerParams(vmem_limit_bytes=vmem * 2**20),
        **kw,
    )(*args)


def flat(a):
    return jnp.concatenate([a[r : r + 1, :] for r in range(a.shape[0])], axis=1)


def push_kernel(
    owners,
    cap,
    chunk,
    target_hbm,
    offset_hbm,
    observed_hbm,
    flags_hbm,
    out_hbm,
    target_ref,
    offset_ref,
    observed_ref,
    flags_ref,
    data,
    staged,
    sems,
    out_sems,
):
    pairs = (
        (target_hbm, target_ref),
        (offset_hbm, offset_ref),
        (observed_hbm, observed_ref),
        (flags_hbm, flags_ref),
    )
    gets = [pltpu.make_async_copy(src, dst, sems.at[k]) for k, (src, dst) in enumerate(pairs)]
    for get in gets:
        get.start()
    gets[0].wait()
    gets[1].wait()
    tiles = target_ref.shape[0]
    count = tiles * LANES
    channels = observed_ref.shape[1]
    owner = flat(target_ref[...])
    places = lax.axis_size("zhi")
    near = owners // places
    shift = (owner // near - lax.axis_index("zhi") + places) & (places - 1)
    ring = (shift - 2 * (owner & 1) + places) & (places - 1)
    swap = jnp.where(shift == places // 2, near // 2, 0)
    target = ((owner & (near - 1)) ^ swap) * places + ring
    offset = flat(offset_ref[...])
    hot = jnp.where(iota((owners, count), 0) == target, 1.0, 0.0)
    upper = jnp.where(iota((256, 256), 0) <= iota((256, 256), 1), 1.0, 0.0).astype(BF16)
    carry = jnp.zeros((owners, 1), F32)
    slots = []
    for b in range(count // 256):
        part = hot[:, b * 256 : (b + 1) * 256]
        seen = nn(part.astype(BF16), upper) + carry
        carry = seen[:, 255:256]
        slots.append(jnp.sum(part * (seen - 1.0), axis=0, keepdims=True))
    slot = jnp.concatenate(slots, axis=1)
    place = target * cap + slot.astype(jnp.int32)
    high = offset // BASE
    low = offset - high * BASE
    at_slot = jnp.where((iota((LANES, count), 0) & (cap - 1)).astype(F32) == slot, 1.0, 0.0)
    hot = hot.astype(BF16)
    pair = jnp.concatenate([at_slot * (high + 1).astype(F32), at_slot * low.astype(F32)], axis=0)
    pair = nt(hot, pair.astype(BF16))
    high, low = pair[:, :LANES] - 1.0, pair[:, LANES:]

    gets[2].wait()
    data[:, :channels] = observed_ref[...].astype(BF16)
    gets[3].wait()
    data[:, channels:] = flags_ref[...].astype(F32).astype(BF16)
    parts = 2 * channels // LANES
    puts = []
    for k, s in enumerate(range(0, owners, chunk)):
        put = jnp.where(place - s * cap == iota((chunk * cap, count), 0), 1.0, 0.0).astype(BF16)
        rows = nn(put, data[...]).astype(BF16).reshape(chunk, cap, 2 * channels)
        for j in range(parts):
            staged[s : s + chunk, j * cap : (j + 1) * cap, :] = rows[:, :, j * LANES : (j + 1) * LANES]
        digits = jnp.where(
            iota((chunk, 8, LANES), 1) == 0,
            high[s : s + chunk, :].reshape(chunk, 1, LANES),
            low[s : s + chunk, :].reshape(chunk, 1, LANES),
        )
        staged[s : s + chunk, parts * cap :, :] = digits.astype(BF16)
        puts.append(
            pltpu.make_async_copy(
                staged.at[pl.ds(s, chunk)], out_hbm.at[pl.ds(s, chunk)], out_sems.at[k]
            )
        )
        puts[-1].start()
    for put in puts:
        put.wait()


def forward_kernel(table_ref, w1_ref, w2_ref, w3_ref, evolved_ref, first_ref, second_ref):
    first = jnp.tanh(nn(table_ref[...], w1_ref[...])).astype(BF16)
    second = jnp.tanh(nn(first, w2_ref[...])).astype(BF16)
    first_ref[...] = first
    second_ref[...] = second
    evolved_ref[...] = nn(second, w3_ref[...]).astype(BF16)


def departures_kernel(cap, chunk, arrived_ref, evolved_ref, sigma_ref, out_ref, ids_ref):
    sources = arrived_ref.shape[0]
    cols, channels = evolved_ref.shape
    parts = channels // LANES
    digits = arrived_ref[:, 2 * parts * cap :, :].reshape(sources * 8, LANES)
    row = iota((sources, sources * 8), 1) - 8 * iota((sources, sources * 8), 0)
    high = nn(jnp.where(row == 0, 1.0, 0.0).astype(BF16), digits)
    low = nn(jnp.where(row == 1, 1.0, 0.0).astype(BF16), digits)
    per = LANES // cap
    mine = iota((sources, LANES), 1) // cap == iota((sources, LANES), 0) % per
    gather = jnp.where(
        iota((sources // per, sources), 1) // per == iota((sources // per, sources), 0), 1.0, 0.0
    ).astype(BF16)
    spread = lambda a: nn(gather, jnp.where(mine, a, 0.0).astype(BF16))
    ids_ref[...] = (spread(high) * BASE + spread(low)).astype(jnp.int32)
    column = (high * BASE + low).T
    wide = iota((cap, cols), 1).astype(F32)
    inverse = 1.0 / sigma_ref[...]
    for s in range(0, sources, chunk):
        pick = jnp.concatenate(
            [
                jnp.where(column[:cap, s + j : s + j + 1] == wide, 1.0, 0.0).astype(BF16)
                for j in range(chunk)
            ],
            axis=0,
        )
        evolved = nn(pick, evolved_ref[...])
        for j in range(parts):
            lanes = slice(j * LANES, (j + 1) * LANES)
            take = lambda k: arrived_ref[s : s + chunk, k * cap : (k + 1) * cap, :].reshape(
                chunk * cap, LANES
            ).astype(F32)
            departure = (evolved[:, lanes] - take(j)) * inverse[:, lanes]
            weighted = take(parts + j) * jnp.clip(departure, -1.5, 1.5) * inverse[:, lanes]
            out_ref[s * cap : (s + chunk) * cap, lanes] = weighted.astype(BF16)


def adjoint_kernel(
    shifts, quarter, ids_ref, departures_ref, first_ref, second_ref, w1_ref, w2_ref, w3_ref, *outs
):
    groups = len(shifts)
    each = range(groups)
    which = [lax.rem(lax.axis_index("chan") + k, groups) * quarter for k in shifts]
    rows = [pl.ds(pl.multiple_of(start, quarter), quarter) for start in which]
    ids = flat(ids_ref[...])
    total, grad_second, grad_first = [], [], []
    for k in each:
        put = jnp.where(ids - which[k] == iota((quarter, ids.shape[1]), 0), 1.0, 0.0).astype(BF16)
        total.append(nn(put, departures_ref[...]).astype(BF16))
    for k in each:
        second = second_ref[rows[k], :].astype(F32)
        grad_second.append((nt(total[k], w3_ref[...]) * (1.0 - second * second)).astype(BF16))
    for k in each:
        first = first_ref[rows[k], :].astype(F32)
        grad_first.append((nt(grad_second[k], w2_ref[...]) * (1.0 - first * first)).astype(BF16))
    part = quarter // PACK
    lane = iota((part, LANES), 1) // SPAN
    for k, out_ref in enumerate(outs):
        grads = nt(grad_first[k], w1_ref[...])
        out_ref[:quarter, :] = grads[:, :LANES].astype(BF16)
        out_ref[quarter : 2 * quarter, :] = grads[:, LANES : 2 * LANES].astype(BF16)
        tail = grads[:, 2 * LANES :]
        packed = tail[:part, :]
        for g in range(1, PACK):
            packed = jnp.where(
                lane == g, pltpu.roll(tail[g * part : (g + 1) * part, :], g * SPAN, 1), packed
            )
        out_ref[2 * quarter :, :] = packed.astype(BF16)


def add_kernel(so_far_ref, part_ref, out_ref):
    out_ref[...] = so_far_ref[...].astype(F32) + part_ref[...].astype(F32)


def total_kernel(so_far_ref, part_ref, out_ref):
    width, quarter = out_ref.shape
    total = so_far_ref[...] + part_ref[...].astype(F32)
    packed = total[2 * quarter :]
    tail = jnp.concatenate(
        [packed] + [pltpu.roll(packed, LANES - g * SPAN, 1) for g in range(1, PACK)], axis=0
    )
    out_ref[:LANES, :] = total[:quarter].T
    out_ref[LANES : 2 * LANES, :] = total[quarter : 2 * quarter].T
    out_ref[2 * LANES :, :] = tail.T[: width - 2 * LANES, :]


def on_device(
    profiles, owner_block, column_offset, observed, sigma, qc_flags, w_first, w_second, w_third
):
    sizes = tuple(lax.axis_size(name) for name in AXES)
    owners = math.prod(sizes[:-1])
    places, groups = sizes[0], sizes[-1]
    everyone = devices(sizes)
    number = {place: i for i, place in enumerate(everyone)}
    rows = owner_block.shape[0]
    cap = 2 * rows // owners
    cols, width = profiles.shape
    hidden, channels = w_third.shape
    quarter = cols // groups
    tiles = rows // LANES
    chunk = 16
    few = 8
    sds = jax.ShapeDtypeStruct
    far = pl.BlockSpec(memory_space=pltpu.HBM)

    def at_home(place, chan):
        return number[(*home(place, places), chan)]

    fetched = lax.ppermute(profiles.T, AXES, [(at_home(p, p[4]), number[p]) for p in everyone])

    bundle = sds((owners, 2 * channels // LANES * cap + 8, LANES), BF16)
    pushed = call(
        functools.partial(push_kernel, owners, cap, few),
        bundle,
        (owner_block.reshape(tiles, LANES), column_offset.reshape(tiles, LANES), observed, qc_flags),
        vmem=62,
        in_specs=[far] * 4,
        out_specs=far,
        scratch_shapes=[
            pltpu.VMEM((tiles, LANES), jnp.int32),
            pltpu.VMEM((tiles, LANES), jnp.int32),
            pltpu.VMEM((rows, channels), F32),
            pltpu.VMEM((rows, channels), jnp.int32),
            pltpu.VMEM((rows, 2 * channels), BF16),
            pltpu.VMEM(bundle.shape, BF16),
            pltpu.SemaphoreType.DMA((4,)),
            pltpu.SemaphoreType.DMA((owners // few,)),
        ],
    )
    arrived = lax.all_to_all(pushed, GROUP, split_axis=0, concat_axis=0, tiled=True)

    padded = -(-width // LANES) * LANES
    wide = lambda a, axis: jnp.pad(a, [(0, padded - width) if k == axis else (0, 0) for k in (0, 1)])
    w1 = wide(w_first, 0)
    evolved, first, second = call(
        forward_kernel,
        (sds((cols, channels), BF16), sds((cols, hidden), BF16), sds((cols, hidden), BF16)),
        (wide(fetched.T, 1), w1, w_second, w_third),
        vmem=24,
        cost_estimate=pl.CostEstimate(flops=10**11, bytes_accessed=4 * 10**6, transcendentals=10**6),
    )

    departures, ids = call(
        functools.partial(departures_kernel, cap, chunk),
        (sds((owners * cap, channels), BF16), sds((owners * cap // LANES, LANES), jnp.int32)),
        (arrived, evolved, sigma.reshape(1, channels)),
        vmem=32,
    )
    order = sorted(range(groups), key=lambda k: -min(k, groups - k))
    gradients = call(
        functools.partial(adjoint_kernel, order, quarter),
        [sds((2 * quarter + quarter // PACK, LANES), BF16)] * groups,
        (ids, departures, first, second, w1, w_second, w_third),
        vmem=32,
        cost_estimate=pl.CostEstimate(flops=8 * 10**9, bytes_accessed=4 * 10**6, transcendentals=0),
    )
    shares = [
        lax.ppermute(part, AXES, [(number[p], at_home(p, (p[4] + k) % groups)) for p in everyone])
        for k, part in zip(order, gradients)
    ]
    total = shares[0]
    for share in shares[1:-1]:
        total = call(
            add_kernel,
            sds(share.shape, F32),
            (total, share),
            vmem=24,
            cost_estimate=pl.CostEstimate(flops=10**10, bytes_accessed=10**6, transcendentals=0),
        )
    return call(total_kernel, sds((width, quarter), F32), (total, shares[-1]), vmem=24).T


def solution(mesh):
    grid, chan = mesh.devices.shape
    places = 4
    near = jax.sharding.Mesh(mesh.devices.reshape(places, 2, grid // (4 * places), 2, chan), AXES)
    whole = P((*GRID, "chan"), None)
    in_specs = (P(GRID, None), whole, P((*GRID, "chan")), whole, P(), whole, P(), P(), P())
    return jax.shard_map(on_device, mesh=near, in_specs=in_specs, out_specs=whole, check_vma=False)
```

```python
import functools
import itertools
import math

import jax
import jax.numpy as jnp
from jax import lax
from jax.experimental import pallas as pl
from jax.experimental.pallas import tpu as pltpu
from jax.sharding import PartitionSpec as P

LANES = 128
BASE = 32
AXES = ("zhi", "zlo", "y", "core", "chan")
GROUP = AXES[1:]
GRID = AXES[:-1]


def home(place, places):
    zhi, zlo, y, core, chan = place
    shift = (chan + 2 * core) % places
    return (zhi + shift) % places, zlo ^ int(shift == places // 2), y, core


def devices(sizes):
    return list(itertools.product(*(range(n) for n in sizes)))
F32 = jnp.float32
BF16 = jnp.bfloat16
NT = (((1,), (1,)), ((), ()))


def iota(shape, axis):
    return lax.broadcasted_iota(jnp.int32, shape, axis)


def nn(a, b):
    return jnp.dot(a, b, preferred_element_type=F32)


def nt(a, b):
    return lax.dot_general(a, b, NT, preferred_element_type=F32)


def call(kernel, out, args, vmem=48, **kw):
    return pl.pallas_call(
        kernel,
        out_shape=out,
        compiler_params=pltpu.CompilerParams(vmem_limit_bytes=vmem * 2**20),
        **kw,
    )(*args)


def flat(a):
    return jnp.concatenate([a[r : r + 1, :] for r in range(a.shape[0])], axis=1)


def push_kernel(
    owners,
    cap,
    chunk,
    target_hbm,
    offset_hbm,
    observed_hbm,
    flags_hbm,
    out_hbm,
    target_ref,
    offset_ref,
    observed_ref,
    flags_ref,
    data,
    staged,
    sems,
    out_sems,
):
    pairs = (
        (target_hbm, target_ref),
        (offset_hbm, offset_ref),
        (observed_hbm, observed_ref),
        (flags_hbm, flags_ref),
    )
    gets = [pltpu.make_async_copy(src, dst, sems.at[k]) for k, (src, dst) in enumerate(pairs)]
    for get in gets:
        get.start()
    gets[0].wait()
    gets[1].wait()
    tiles = target_ref.shape[0]
    count = tiles * LANES
    channels = observed_ref.shape[1]
    owner = flat(target_ref[...])
    places = lax.axis_size("zhi")
    near = owners // places
    shift = (owner // near - lax.axis_index("zhi") + places) & (places - 1)
    ring = (shift - 2 * (owner & 1) + places) & (places - 1)
    swap = jnp.where(shift == places // 2, near // 2, 0)
    target = ((owner & (near - 1)) ^ swap) * places + ring
    offset = flat(offset_ref[...])
    hot = jnp.where(iota((owners, count), 0) == target, 1.0, 0.0)
    upper = jnp.where(iota((256, 256), 0) <= iota((256, 256), 1), 1.0, 0.0).astype(BF16)
    carry = jnp.zeros((owners, 1), F32)
    slots = []
    for b in range(count // 256):
        part = hot[:, b * 256 : (b + 1) * 256]
        seen = nn(part.astype(BF16), upper) + carry
        carry = seen[:, 255:256]
        slots.append(jnp.sum(part * (seen - 1.0), axis=0, keepdims=True))
    slot = jnp.concatenate(slots, axis=1)
    place = target * cap + slot.astype(jnp.int32)
    high = offset // BASE
    low = offset - high * BASE
    at_slot = jnp.where((iota((LANES, count), 0) & (cap - 1)).astype(F32) == slot, 1.0, 0.0)
    hot = hot.astype(BF16)
    pair = jnp.concatenate([at_slot * (high + 1).astype(F32), at_slot * low.astype(F32)], axis=0)
    pair = nt(hot, pair.astype(BF16))
    high, low = pair[:, :LANES] - 1.0, pair[:, LANES:]

    gets[2].wait()
    data[:, :channels] = observed_ref[...].astype(BF16)
    gets[3].wait()
    data[:, channels:] = flags_ref[...].astype(F32).astype(BF16)
    parts = 2 * channels // LANES
    puts = []
    for k, s in enumerate(range(0, owners, chunk)):
        put = jnp.where(place - s * cap == iota((chunk * cap, count), 0), 1.0, 0.0).astype(BF16)
        rows = nn(put, data[...]).astype(BF16).reshape(chunk, cap, 2 * channels)
        for j in range(parts):
            staged[s : s + chunk, j * cap : (j + 1) * cap, :] = rows[:, :, j * LANES : (j + 1) * LANES]
        digits = jnp.where(
            iota((chunk, 8, LANES), 1) == 0,
            high[s : s + chunk, :].reshape(chunk, 1, LANES),
            low[s : s + chunk, :].reshape(chunk, 1, LANES),
        )
        staged[s : s + chunk, parts * cap :, :] = digits.astype(BF16)
        puts.append(
            pltpu.make_async_copy(
                staged.at[pl.ds(s, chunk)], out_hbm.at[pl.ds(s, chunk)], out_sems.at[k]
            )
        )
        puts[-1].start()
    for put in puts:
        put.wait()


def forward_kernel(table_ref, w1_ref, w2_ref, w3_ref, evolved_ref, first_ref, second_ref):
    first = jnp.tanh(nn(table_ref[...], w1_ref[...])).astype(BF16)
    second = jnp.tanh(nn(first, w2_ref[...])).astype(BF16)
    first_ref[...] = first
    second_ref[...] = second
    evolved_ref[...] = nn(second, w3_ref[...]).astype(BF16)


def departures_kernel(cap, chunk, arrived_ref, evolved_ref, sigma_ref, out_ref, ids_ref):
    sources = arrived_ref.shape[0]
    cols, channels = evolved_ref.shape
    parts = channels // LANES
    digits = arrived_ref[:, 2 * parts * cap :, :].reshape(sources * 8, LANES)
    row = iota((sources, sources * 8), 1) - 8 * iota((sources, sources * 8), 0)
    high = nn(jnp.where(row == 0, 1.0, 0.0).astype(BF16), digits)
    low = nn(jnp.where(row == 1, 1.0, 0.0).astype(BF16), digits)
    per = LANES // cap
    mine = iota((sources, LANES), 1) // cap == iota((sources, LANES), 0) % per
    gather = jnp.where(
        iota((sources // per, sources), 1) // per == iota((sources // per, sources), 0), 1.0, 0.0
    ).astype(BF16)
    spread = lambda a: nn(gather, jnp.where(mine, a, 0.0).astype(BF16))
    ids_ref[...] = (spread(high) * BASE + spread(low)).astype(jnp.int32)
    column = (high * BASE + low).T
    wide = iota((cap, cols), 1).astype(F32)
    inverse = 1.0 / sigma_ref[...]
    for s in range(0, sources, chunk):
        pick = jnp.concatenate(
            [
                jnp.where(column[:cap, s + j : s + j + 1] == wide, 1.0, 0.0).astype(BF16)
                for j in range(chunk)
            ],
            axis=0,
        )
        evolved = nn(pick, evolved_ref[...])
        for j in range(parts):
            lanes = slice(j * LANES, (j + 1) * LANES)
            take = lambda k: arrived_ref[s : s + chunk, k * cap : (k + 1) * cap, :].reshape(
                chunk * cap, LANES
            ).astype(F32)
            departure = (evolved[:, lanes] - take(j)) * inverse[:, lanes]
            weighted = take(parts + j) * jnp.clip(departure, -1.5, 1.5) * inverse[:, lanes]
            out_ref[s * cap : (s + chunk) * cap, lanes] = weighted.astype(BF16)


def adjoint_kernel(
    shifts, quarter, ids_ref, departures_ref, first_ref, second_ref, w1_ref, w2_ref, w3_ref, *outs
):
    groups = len(shifts)
    each = range(groups)
    which = [lax.rem(lax.axis_index("chan") + k, groups) * quarter for k in shifts]
    rows = [pl.ds(pl.multiple_of(start, quarter), quarter) for start in which]
    ids = flat(ids_ref[...])
    total, grad_second, grad_first = [], [], []
    for k in each:
        put = jnp.where(ids - which[k] == iota((quarter, ids.shape[1]), 0), 1.0, 0.0).astype(BF16)
        total.append(nn(put, departures_ref[...]).astype(BF16))
    for k in each:
        second = second_ref[rows[k], :].astype(F32)
        grad_second.append((nt(total[k], w3_ref[...]) * (1.0 - second * second)).astype(BF16))
    for k in each:
        first = first_ref[rows[k], :].astype(F32)
        grad_first.append((nt(grad_second[k], w2_ref[...]) * (1.0 - first * first)).astype(BF16))
    for k, out_ref in enumerate(outs):
        out_ref[...] = nt(w1_ref[: out_ref.shape[0], :], grad_first[k]).astype(BF16)


def add_kernel(so_far_ref, part_ref, out_ref):
    out_ref[...] = so_far_ref[...].astype(F32) + part_ref[...].astype(F32)


def total_kernel(so_far_ref, part_ref, out_ref):
    total = so_far_ref[...] + part_ref[...].astype(F32)
    out_ref[...] = total[: out_ref.shape[0], :]


def on_device(
    profiles, owner_block, column_offset, observed, sigma, qc_flags, w_first, w_second, w_third
):
    sizes = tuple(lax.axis_size(name) for name in AXES)
    owners = math.prod(sizes[:-1])
    places, groups = sizes[0], sizes[-1]
    everyone = devices(sizes)
    number = {place: i for i, place in enumerate(everyone)}
    rows = owner_block.shape[0]
    cap = 2 * rows // owners
    cols, width = profiles.shape
    hidden, channels = w_third.shape
    quarter = cols // groups
    tiles = rows // LANES
    chunk = 16
    few = 8
    sds = jax.ShapeDtypeStruct
    far = pl.BlockSpec(memory_space=pltpu.HBM)

    def at_home(place, chan):
        return number[(*home(place, places), chan)]

    fetched = lax.ppermute(profiles.T, AXES, [(at_home(p, p[4]), number[p]) for p in everyone])

    bundle = sds((owners, 2 * channels // LANES * cap + 8, LANES), BF16)
    pushed = call(
        functools.partial(push_kernel, owners, cap, few),
        bundle,
        (owner_block.reshape(tiles, LANES), column_offset.reshape(tiles, LANES), observed, qc_flags),
        vmem=62,
        in_specs=[far] * 4,
        out_specs=far,
        scratch_shapes=[
            pltpu.VMEM((tiles, LANES), jnp.int32),
            pltpu.VMEM((tiles, LANES), jnp.int32),
            pltpu.VMEM((rows, channels), F32),
            pltpu.VMEM((rows, channels), jnp.int32),
            pltpu.VMEM((rows, 2 * channels), BF16),
            pltpu.VMEM(bundle.shape, BF16),
            pltpu.SemaphoreType.DMA((4,)),
            pltpu.SemaphoreType.DMA((owners // few,)),
        ],
    )
    arrived = lax.all_to_all(pushed, GROUP, split_axis=0, concat_axis=0, tiled=True)

    padded = -(-width // LANES) * LANES
    wide = lambda a, axis: jnp.pad(a, [(0, padded - width) if k == axis else (0, 0) for k in (0, 1)])
    w1 = wide(w_first, 0)
    evolved, first, second = call(
        forward_kernel,
        (sds((cols, channels), BF16), sds((cols, hidden), BF16), sds((cols, hidden), BF16)),
        (wide(fetched.T, 1), w1, w_second, w_third),
        vmem=24,
        cost_estimate=pl.CostEstimate(flops=10**11, bytes_accessed=4 * 10**6, transcendentals=10**6),
    )

    departures, ids = call(
        functools.partial(departures_kernel, cap, chunk),
        (sds((owners * cap, channels), BF16), sds((owners * cap // LANES, LANES), jnp.int32)),
        (arrived, evolved, sigma.reshape(1, channels)),
        vmem=32,
    )
    order = sorted(range(groups), key=lambda k: -min(k, groups - k))
    gradients = call(
        functools.partial(adjoint_kernel, order, quarter),
        [sds((-(-width // 32) * 32, quarter), BF16)] * groups,
        (ids, departures, first, second, w1, w_second, w_third),
        vmem=32,
        cost_estimate=pl.CostEstimate(flops=8 * 10**9, bytes_accessed=4 * 10**6, transcendentals=0),
    )
    shares = [
        lax.ppermute(part, AXES, [(number[p], at_home(p, (p[4] + k) % groups)) for p in everyone])
        for k, part in zip(order, gradients)
    ]
    total = shares[0]
    for share in shares[1:-1]:
        total = call(
            add_kernel,
            sds(share.shape, F32),
            (total, share),
            vmem=24,
            cost_estimate=pl.CostEstimate(flops=10**10, bytes_accessed=10**6, transcendentals=0),
        )
    return call(total_kernel, sds((width, quarter), F32), (total, shares[-1]), vmem=24).T


def solution(mesh):
    grid, chan = mesh.devices.shape
    places = 4
    near = jax.sharding.Mesh(mesh.devices.reshape(places, 2, grid // (4 * places), 2, chan), AXES)
    whole = P((*GRID, "chan"), None)
    in_specs = (P(GRID, None), whole, P((*GRID, "chan")), whole, P(), whole, P(), P(), P())
    return jax.shard_map(on_device, mesh=near, in_specs=in_specs, out_specs=whole, check_vma=False)
```

```python
import functools
import itertools
import math

import jax
import jax.numpy as jnp
from jax import lax
from jax.experimental import pallas as pl
from jax.experimental.pallas import tpu as pltpu
from jax.sharding import PartitionSpec as P

LANES = 128
BASE = 32
AXES = ("zhi", "zlo", "y", "core", "chan")
GROUP = AXES[1:]
GRID = AXES[:-1]


def home(place, places):
    zhi, zlo, y, core, chan = place
    shift = (chan + 2 * core) % places
    return (zhi + shift) % places, zlo ^ int(shift == places // 2), y, core


def devices(sizes):
    return list(itertools.product(*(range(n) for n in sizes)))
F32 = jnp.float32
BF16 = jnp.bfloat16
NT = (((1,), (1,)), ((), ()))


def iota(shape, axis):
    return lax.broadcasted_iota(jnp.int32, shape, axis)


def nn(a, b):
    return jnp.dot(a, b, preferred_element_type=F32)


def nt(a, b):
    return lax.dot_general(a, b, NT, preferred_element_type=F32)


def call(kernel, out, args, vmem=48, **kw):
    return pl.pallas_call(
        kernel,
        out_shape=out,
        compiler_params=pltpu.CompilerParams(vmem_limit_bytes=vmem * 2**20),
        **kw,
    )(*args)


def flat(a):
    return jnp.concatenate([a[r : r + 1, :] for r in range(a.shape[0])], axis=1)


def push_kernel(
    owners,
    cap,
    chunk,
    target_hbm,
    offset_hbm,
    observed_hbm,
    flags_hbm,
    out_hbm,
    target_ref,
    offset_ref,
    observed_ref,
    flags_ref,
    data,
    staged,
    sems,
    out_sems,
):
    pairs = (
        (target_hbm, target_ref),
        (offset_hbm, offset_ref),
        (observed_hbm, observed_ref),
        (flags_hbm, flags_ref),
    )
    gets = [pltpu.make_async_copy(src, dst, sems.at[k]) for k, (src, dst) in enumerate(pairs)]
    for get in gets:
        get.start()
    gets[0].wait()
    gets[1].wait()
    tiles = target_ref.shape[0]
    count = tiles * LANES
    channels = observed_ref.shape[1]
    owner = flat(target_ref[...])
    places = lax.axis_size("zhi")
    near = owners // places
    shift = (owner // near - lax.axis_index("zhi") + places) & (places - 1)
    ring = (shift - 2 * (owner & 1) + places) & (places - 1)
    swap = jnp.where(shift == places // 2, near // 2, 0)
    target = ((owner & (near - 1)) ^ swap) * places + ring
    offset = flat(offset_ref[...])
    hot = jnp.where(iota((owners, count), 0) == target, 1.0, 0.0)
    upper = jnp.where(iota((256, 256), 0) <= iota((256, 256), 1), 1.0, 0.0).astype(BF16)
    carry = jnp.zeros((owners, 1), F32)
    slots = []
    for b in range(count // 256):
        part = hot[:, b * 256 : (b + 1) * 256]
        seen = nn(part.astype(BF16), upper) + carry
        carry = seen[:, 255:256]
        slots.append(jnp.sum(part * (seen - 1.0), axis=0, keepdims=True))
    slot = jnp.concatenate(slots, axis=1)
    place = target * cap + slot.astype(jnp.int32)
    high = offset // BASE
    low = offset - high * BASE
    at_slot = jnp.where((iota((LANES, count), 0) & (cap - 1)).astype(F32) == slot, 1.0, 0.0)
    hot = hot.astype(BF16)
    pair = jnp.concatenate([at_slot * (high + 1).astype(F32), at_slot * low.astype(F32)], axis=0)
    pair = nt(hot, pair.astype(BF16))
    high, low = pair[:, :LANES] - 1.0, pair[:, LANES:]

    gets[2].wait()
    data[:, :channels] = observed_ref[...].astype(BF16)
    gets[3].wait()
    data[:, channels:] = flags_ref[...].astype(F32).astype(BF16)
    parts = 2 * channels // LANES
    puts = []
    for k, s in enumerate(range(0, owners, chunk)):
        put = jnp.where(place - s * cap == iota((chunk * cap, count), 0), 1.0, 0.0).astype(BF16)
        rows = nn(put, data[...]).astype(BF16).reshape(chunk, cap, 2 * channels)
        for j in range(parts):
            staged[s : s + chunk, j * cap : (j + 1) * cap, :] = rows[:, :, j * LANES : (j + 1) * LANES]
        digits = jnp.where(
            iota((chunk, 8, LANES), 1) == 0,
            high[s : s + chunk, :].reshape(chunk, 1, LANES),
            low[s : s + chunk, :].reshape(chunk, 1, LANES),
        )
        staged[s : s + chunk, parts * cap :, :] = digits.astype(BF16)
        puts.append(
            pltpu.make_async_copy(
                staged.at[pl.ds(s, chunk)], out_hbm.at[pl.ds(s, chunk)], out_sems.at[k]
            )
        )
        puts[-1].start()
    for put in puts:
        put.wait()


def forward_kernel(table_ref, w1_ref, w2_ref, w3_ref, evolved_ref, first_ref, second_ref):
    first = jnp.tanh(nn(table_ref[...], w1_ref[...])).astype(BF16)
    second = jnp.tanh(nn(first, w2_ref[...])).astype(BF16)
    first_ref[...] = first
    second_ref[...] = second
    evolved_ref[...] = nn(second, w3_ref[...]).astype(BF16)


def decode_kernel(cap, parts, arrived_ref, ids_ref, column_ref):
    sources = arrived_ref.shape[0]
    digits = arrived_ref[:, 2 * parts * cap :, :].reshape(sources * 8, LANES)
    row = iota((sources, sources * 8), 1) - 8 * iota((sources, sources * 8), 0)
    high = nn(jnp.where(row == 0, 1.0, 0.0).astype(BF16), digits)
    low = nn(jnp.where(row == 1, 1.0, 0.0).astype(BF16), digits)
    per = LANES // cap
    mine = iota((sources, LANES), 1) // cap == iota((sources, LANES), 0) % per
    gather = jnp.where(
        iota((sources // per, sources), 1) // per == iota((sources // per, sources), 0), 1.0, 0.0
    ).astype(BF16)
    spread = lambda a: nn(gather, jnp.where(mine, a, 0.0).astype(BF16))
    ids_ref[...] = (spread(high) * BASE + spread(low)).astype(jnp.int32)
    column_ref[...] = (high * BASE + low).T[:cap, :]


def departures_kernel(cap, chunk, arrived_ref, column_ref, evolved_ref, sigma_ref, out_ref):
    sources = arrived_ref.shape[0]
    cols, channels = evolved_ref.shape
    parts = channels // LANES
    column = column_ref[...]
    wide = iota((cap, cols), 1).astype(F32)
    inverse = 1.0 / sigma_ref[...]
    for s in range(0, sources, chunk):
        pick = jnp.concatenate(
            [
                jnp.where(column[:, s + j : s + j + 1] == wide, 1.0, 0.0).astype(BF16)
                for j in range(chunk)
            ],
            axis=0,
        )
        evolved = nn(pick, evolved_ref[...])
        for j in range(parts):
            lanes = slice(j * LANES, (j + 1) * LANES)
            take = lambda k: arrived_ref[s : s + chunk, k * cap : (k + 1) * cap, :].reshape(
                chunk * cap, LANES
            ).astype(F32)
            departure = (evolved[:, lanes] - take(j)) * inverse[:, lanes]
            weighted = take(parts + j) * jnp.clip(departure, -1.5, 1.5) * inverse[:, lanes]
            out_ref[s * cap : (s + chunk) * cap, lanes] = weighted.astype(BF16)


def adjoint_kernel(
    shifts, quarter, ids_ref, departures_ref, first_ref, second_ref, w1_ref, w2_ref, w3_ref, *outs
):
    groups = len(shifts)
    each = range(groups)
    which = [lax.rem(lax.axis_index("chan") + k, groups) * quarter for k in shifts]
    rows = [pl.ds(pl.multiple_of(start, quarter), quarter) for start in which]
    ids = flat(ids_ref[...])
    total, grad_second, grad_first = [], [], []
    for k in each:
        put = jnp.where(ids - which[k] == iota((quarter, ids.shape[1]), 0), 1.0, 0.0).astype(BF16)
        total.append(nn(put, departures_ref[...]).astype(BF16))
    for k in each:
        second = second_ref[rows[k], :].astype(F32)
        grad_second.append((nt(total[k], w3_ref[...]) * (1.0 - second * second)).astype(BF16))
    for k in each:
        first = first_ref[rows[k], :].astype(F32)
        grad_first.append((nt(grad_second[k], w2_ref[...]) * (1.0 - first * first)).astype(BF16))
    for k, out_ref in enumerate(outs):
        out_ref[...] = nt(w1_ref[: out_ref.shape[0], :], grad_first[k]).astype(BF16)


def add_kernel(so_far_ref, part_ref, out_ref):
    out_ref[...] = so_far_ref[...].astype(F32) + part_ref[...].astype(F32)


def total_kernel(so_far_ref, part_ref, out_ref):
    total = so_far_ref[...] + part_ref[...].astype(F32)
    out_ref[...] = total[: out_ref.shape[0], :]


def on_device(
    profiles, owner_block, column_offset, observed, sigma, qc_flags, w_first, w_second, w_third
):
    sizes = tuple(lax.axis_size(name) for name in AXES)
    owners = math.prod(sizes[:-1])
    places, groups = sizes[0], sizes[-1]
    everyone = devices(sizes)
    number = {place: i for i, place in enumerate(everyone)}
    rows = owner_block.shape[0]
    cap = 2 * rows // owners
    cols, width = profiles.shape
    hidden, channels = w_third.shape
    quarter = cols // groups
    tiles = rows // LANES
    chunk = 16
    few = 8
    sds = jax.ShapeDtypeStruct
    far = pl.BlockSpec(memory_space=pltpu.HBM)

    def at_home(place, chan):
        return number[(*home(place, places), chan)]

    fetched = lax.ppermute(profiles.T, AXES, [(at_home(p, p[4]), number[p]) for p in everyone])

    bundle = sds((owners, 2 * channels // LANES * cap + 8, LANES), BF16)
    pushed = call(
        functools.partial(push_kernel, owners, cap, few),
        bundle,
        (owner_block.reshape(tiles, LANES), column_offset.reshape(tiles, LANES), observed, qc_flags),
        vmem=62,
        in_specs=[far] * 4,
        out_specs=far,
        scratch_shapes=[
            pltpu.VMEM((tiles, LANES), jnp.int32),
            pltpu.VMEM((tiles, LANES), jnp.int32),
            pltpu.VMEM((rows, channels), F32),
            pltpu.VMEM((rows, channels), jnp.int32),
            pltpu.VMEM((rows, 2 * channels), BF16),
            pltpu.VMEM(bundle.shape, BF16),
            pltpu.SemaphoreType.DMA((4,)),
            pltpu.SemaphoreType.DMA((owners // few,)),
        ],
    )
    arrived = lax.all_to_all(pushed, GROUP, split_axis=0, concat_axis=0, tiled=True)

    padded = -(-width // LANES) * LANES
    wide = lambda a, axis: jnp.pad(a, [(0, padded - width) if k == axis else (0, 0) for k in (0, 1)])
    w1 = wide(w_first, 0)
    evolved, first, second = call(
        forward_kernel,
        (sds((cols, channels), BF16), sds((cols, hidden), BF16), sds((cols, hidden), BF16)),
        (wide(fetched.T, 1), w1, w_second, w_third),
        vmem=24,
        cost_estimate=pl.CostEstimate(flops=10**11, bytes_accessed=4 * 10**6, transcendentals=10**6),
    )

    ids, column = call(
        functools.partial(decode_kernel, cap, channels // LANES),
        (sds((owners * cap // LANES, LANES), jnp.int32), sds((cap, owners), F32)),
        (arrived,),
        vmem=32,
        cost_estimate=pl.CostEstimate(flops=2 * 10**9, bytes_accessed=10**5, transcendentals=0),
    )
    departures = call(
        functools.partial(departures_kernel, cap, chunk),
        sds((owners * cap, channels), BF16),
        (arrived, column, evolved, sigma.reshape(1, channels)),
        vmem=32,
    )
    order = sorted(range(groups), key=lambda k: -min(k, groups - k))
    gradients = call(
        functools.partial(adjoint_kernel, order, quarter),
        [sds((-(-width // 32) * 32, quarter), BF16)] * groups,
        (ids, departures, first, second, w1, w_second, w_third),
        vmem=32,
        cost_estimate=pl.CostEstimate(flops=8 * 10**9, bytes_accessed=4 * 10**6, transcendentals=0),
    )
    shares = [
        lax.ppermute(part, AXES, [(number[p], at_home(p, (p[4] + k) % groups)) for p in everyone])
        for k, part in zip(order, gradients)
    ]
    total = shares[0]
    for share in shares[1:-1]:
        total = call(
            add_kernel,
            sds(share.shape, F32),
            (total, share),
            vmem=24,
            cost_estimate=pl.CostEstimate(flops=10**10, bytes_accessed=10**6, transcendentals=0),
        )
    return call(total_kernel, sds((width, quarter), F32), (total, shares[-1]), vmem=24).T


def solution(mesh):
    grid, chan = mesh.devices.shape
    places = 4
    near = jax.sharding.Mesh(mesh.devices.reshape(places, 2, grid // (4 * places), 2, chan), AXES)
    whole = P((*GRID, "chan"), None)
    in_specs = (P(GRID, None), whole, P((*GRID, "chan")), whole, P(), whole, P(), P(), P())
    return jax.shard_map(on_device, mesh=near, in_specs=in_specs, out_specs=whole, check_vma=False)
```

```python
import functools
import itertools
import math

import jax
import jax.numpy as jnp
from jax import lax
from jax.experimental import pallas as pl
from jax.experimental.pallas import tpu as pltpu
from jax.sharding import PartitionSpec as P

LANES = 128
BASE = 32
AXES = ("zhi", "zlo", "y", "core", "chan")
GROUP = AXES[1:]
GRID = AXES[:-1]


def home(place, places):
    zhi, zlo, y, core, chan = place
    shift = (chan + 2 * core) % places
    return (zhi + shift) % places, zlo ^ int(shift == places // 2), y, core


def devices(sizes):
    return list(itertools.product(*(range(n) for n in sizes)))
F32 = jnp.float32
BF16 = jnp.bfloat16
NT = (((1,), (1,)), ((), ()))


def iota(shape, axis):
    return lax.broadcasted_iota(jnp.int32, shape, axis)


def nn(a, b):
    return jnp.dot(a, b, preferred_element_type=F32)


def nt(a, b):
    return lax.dot_general(a, b, NT, preferred_element_type=F32)


def call(kernel, out, args, vmem=48, **kw):
    return pl.pallas_call(
        kernel,
        out_shape=out,
        compiler_params=pltpu.CompilerParams(vmem_limit_bytes=vmem * 2**20),
        **kw,
    )(*args)


def flat(a):
    return jnp.concatenate([a[r : r + 1, :] for r in range(a.shape[0])], axis=1)


def push_kernel(
    owners,
    cap,
    chunk,
    target_hbm,
    offset_hbm,
    observed_hbm,
    flags_hbm,
    out_hbm,
    target_ref,
    offset_ref,
    observed_ref,
    flags_ref,
    data,
    staged,
    sems,
    out_sems,
):
    pairs = (
        (target_hbm, target_ref),
        (offset_hbm, offset_ref),
        (observed_hbm, observed_ref),
        (flags_hbm, flags_ref),
    )
    gets = [pltpu.make_async_copy(src, dst, sems.at[k]) for k, (src, dst) in enumerate(pairs)]
    for get in gets:
        get.start()
    gets[0].wait()
    gets[1].wait()
    tiles = target_ref.shape[0]
    count = tiles * LANES
    channels = observed_ref.shape[1]
    owner = flat(target_ref[...])
    places = lax.axis_size("zhi")
    near = owners // places
    shift = (owner // near - lax.axis_index("zhi") + places) & (places - 1)
    ring = (shift - 2 * (owner & 1) + places) & (places - 1)
    swap = jnp.where(shift == places // 2, near // 2, 0)
    target = ((owner & (near - 1)) ^ swap) * places + ring
    offset = flat(offset_ref[...])
    hot = jnp.where(iota((owners, count), 0) == target, 1.0, 0.0)
    upper = jnp.where(iota((256, 256), 0) <= iota((256, 256), 1), 1.0, 0.0).astype(BF16)
    carry = jnp.zeros((owners, 1), F32)
    slots = []
    for b in range(count // 256):
        part = hot[:, b * 256 : (b + 1) * 256]
        seen = nn(part.astype(BF16), upper) + carry
        carry = seen[:, 255:256]
        slots.append(jnp.sum(part * (seen - 1.0), axis=0, keepdims=True))
    slot = jnp.concatenate(slots, axis=1)
    place = target * cap + slot.astype(jnp.int32)
    high = offset // BASE
    low = offset - high * BASE
    at_slot = jnp.where((iota((LANES, count), 0) & (cap - 1)).astype(F32) == slot, 1.0, 0.0)
    hot = hot.astype(BF16)
    pair = jnp.concatenate([at_slot * (high + 1).astype(F32), at_slot * low.astype(F32)], axis=0)
    pair = nt(hot, pair.astype(BF16))
    high, low = pair[:, :LANES] - 1.0, pair[:, LANES:]

    gets[2].wait()
    data[:, :channels] = observed_ref[...].astype(BF16)
    gets[3].wait()
    data[:, channels:] = flags_ref[...].astype(F32).astype(BF16)
    parts = 2 * channels // LANES
    puts = []
    for k, s in enumerate(range(0, owners, chunk)):
        put = jnp.where(place - s * cap == iota((chunk * cap, count), 0), 1.0, 0.0).astype(BF16)
        rows = nn(put, data[...]).astype(BF16).reshape(chunk, cap, 2 * channels)
        for j in range(parts):
            staged[s : s + chunk, j * cap : (j + 1) * cap, :] = rows[:, :, j * LANES : (j + 1) * LANES]
        digits = jnp.where(
            iota((chunk, 8, LANES), 1) == 0,
            high[s : s + chunk, :].reshape(chunk, 1, LANES),
            low[s : s + chunk, :].reshape(chunk, 1, LANES),
        )
        staged[s : s + chunk, parts * cap :, :] = digits.astype(BF16)
        puts.append(
            pltpu.make_async_copy(
                staged.at[pl.ds(s, chunk)], out_hbm.at[pl.ds(s, chunk)], out_sems.at[k]
            )
        )
        puts[-1].start()
    for put in puts:
        put.wait()


def forward_kernel(table_ref, w1_ref, w2_ref, w3_ref, evolved_ref, first_ref, second_ref):
    first = jnp.tanh(nn(table_ref[...], w1_ref[...])).astype(BF16)
    second = jnp.tanh(nn(first, w2_ref[...])).astype(BF16)
    first_ref[...] = first
    second_ref[...] = second
    evolved_ref[...] = nn(second, w3_ref[...]).astype(BF16)


def one_hot(cap, column, sources, cols):
    wide = iota((cap, cols), 1).astype(F32)
    picks = [jnp.where(column[:, s : s + 1] == wide, 1.0, 0.0).astype(BF16) for s in sources]
    return jnp.concatenate(picks, axis=0)


def decode_kernel(cap, chunk, parts, arrived_ref, ids_ref, column_ref, pick_ref):
    sources = arrived_ref.shape[0]
    digits = arrived_ref[:, 2 * parts * cap :, :].reshape(sources * 8, LANES)
    row = iota((sources, sources * 8), 1) - 8 * iota((sources, sources * 8), 0)
    high = nn(jnp.where(row == 0, 1.0, 0.0).astype(BF16), digits)
    low = nn(jnp.where(row == 1, 1.0, 0.0).astype(BF16), digits)
    per = LANES // cap
    mine = iota((sources, LANES), 1) // cap == iota((sources, LANES), 0) % per
    gather = jnp.where(
        iota((sources // per, sources), 1) // per == iota((sources // per, sources), 0), 1.0, 0.0
    ).astype(BF16)
    spread = lambda a: nn(gather, jnp.where(mine, a, 0.0).astype(BF16))
    ids_ref[...] = (spread(high) * BASE + spread(low)).astype(jnp.int32)
    column = (high * BASE + low).T[:cap, :]
    column_ref[...] = column
    count, cols = pick_ref.shape
    for s in range(0, count // cap, chunk):
        pick_ref[s * cap : (s + chunk) * cap, :] = one_hot(cap, column, range(s, s + chunk), cols)


def departures_kernel(
    cap, chunk, arrived_ref, column_ref, pick_ref, evolved_ref, sigma_ref, out_ref
):
    sources = arrived_ref.shape[0]
    cols, channels = evolved_ref.shape
    parts = channels // LANES
    column = column_ref[...]
    inverse = 1.0 / sigma_ref[...]
    for s in range(0, sources, chunk):
        if s * cap < pick_ref.shape[0]:
            pick = pick_ref[s * cap : (s + chunk) * cap, :]
        else:
            pick = one_hot(cap, column, range(s, s + chunk), cols)
        evolved = nn(pick, evolved_ref[...])
        for j in range(parts):
            lanes = slice(j * LANES, (j + 1) * LANES)
            take = lambda k: arrived_ref[s : s + chunk, k * cap : (k + 1) * cap, :].reshape(
                chunk * cap, LANES
            ).astype(F32)
            departure = (evolved[:, lanes] - take(j)) * inverse[:, lanes]
            weighted = take(parts + j) * jnp.clip(departure, -1.5, 1.5) * inverse[:, lanes]
            out_ref[s * cap : (s + chunk) * cap, lanes] = weighted.astype(BF16)


def adjoint_kernel(
    shifts, quarter, ids_ref, departures_ref, first_ref, second_ref, w1_ref, w2_ref, w3_ref, *outs
):
    groups = len(shifts)
    each = range(groups)
    which = [lax.rem(lax.axis_index("chan") + k, groups) * quarter for k in shifts]
    rows = [pl.ds(pl.multiple_of(start, quarter), quarter) for start in which]
    ids = flat(ids_ref[...])
    total, grad_second, grad_first = [], [], []
    for k in each:
        put = jnp.where(ids - which[k] == iota((quarter, ids.shape[1]), 0), 1.0, 0.0).astype(BF16)
        total.append(nn(put, departures_ref[...]).astype(BF16))
    for k in each:
        second = second_ref[rows[k], :].astype(F32)
        grad_second.append((nt(total[k], w3_ref[...]) * (1.0 - second * second)).astype(BF16))
    for k in each:
        first = first_ref[rows[k], :].astype(F32)
        grad_first.append((nt(grad_second[k], w2_ref[...]) * (1.0 - first * first)).astype(BF16))
    for k, out_ref in enumerate(outs):
        out_ref[...] = nt(w1_ref[: out_ref.shape[0], :], grad_first[k]).astype(BF16)


def add_kernel(so_far_ref, part_ref, out_ref):
    out_ref[...] = so_far_ref[...].astype(F32) + part_ref[...].astype(F32)


def total_kernel(so_far_ref, part_ref, out_ref):
    total = so_far_ref[...] + part_ref[...].astype(F32)
    out_ref[...] = total[: out_ref.shape[0], :]


def on_device(
    profiles, owner_block, column_offset, observed, sigma, qc_flags, w_first, w_second, w_third
):
    sizes = tuple(lax.axis_size(name) for name in AXES)
    owners = math.prod(sizes[:-1])
    places, groups = sizes[0], sizes[-1]
    everyone = devices(sizes)
    number = {place: i for i, place in enumerate(everyone)}
    rows = owner_block.shape[0]
    cap = 2 * rows // owners
    cols, width = profiles.shape
    hidden, channels = w_third.shape
    quarter = cols // groups
    tiles = rows // LANES
    chunk = 16
    few = 8
    sds = jax.ShapeDtypeStruct
    far = pl.BlockSpec(memory_space=pltpu.HBM)

    def at_home(place, chan):
        return number[(*home(place, places), chan)]

    fetched = lax.ppermute(profiles.T, AXES, [(at_home(p, p[4]), number[p]) for p in everyone])

    bundle = sds((owners, 2 * channels // LANES * cap + 8, LANES), BF16)
    pushed = call(
        functools.partial(push_kernel, owners, cap, few),
        bundle,
        (owner_block.reshape(tiles, LANES), column_offset.reshape(tiles, LANES), observed, qc_flags),
        vmem=62,
        in_specs=[far] * 4,
        out_specs=far,
        scratch_shapes=[
            pltpu.VMEM((tiles, LANES), jnp.int32),
            pltpu.VMEM((tiles, LANES), jnp.int32),
            pltpu.VMEM((rows, channels), F32),
            pltpu.VMEM((rows, channels), jnp.int32),
            pltpu.VMEM((rows, 2 * channels), BF16),
            pltpu.VMEM(bundle.shape, BF16),
            pltpu.SemaphoreType.DMA((4,)),
            pltpu.SemaphoreType.DMA((owners // few,)),
        ],
    )
    arrived = lax.all_to_all(pushed, GROUP, split_axis=0, concat_axis=0, tiled=True)

    padded = -(-width // LANES) * LANES
    wide = lambda a, axis: jnp.pad(a, [(0, padded - width) if k == axis else (0, 0) for k in (0, 1)])
    w1 = wide(w_first, 0)
    evolved, first, second = call(
        forward_kernel,
        (sds((cols, channels), BF16), sds((cols, hidden), BF16), sds((cols, hidden), BF16)),
        (wide(fetched.T, 1), w1, w_second, w_third),
        vmem=24,
        cost_estimate=pl.CostEstimate(flops=10**11, bytes_accessed=4 * 10**6, transcendentals=10**6),
    )

    ids, column, pick = call(
        functools.partial(decode_kernel, cap, chunk, channels // LANES),
        (
            sds((owners * cap // LANES, LANES), jnp.int32),
            sds((cap, owners), F32),
            sds((2 * chunk * cap, cols), BF16),
        ),
        (arrived,),
        vmem=32,
        cost_estimate=pl.CostEstimate(flops=2 * 10**9, bytes_accessed=10**5, transcendentals=0),
    )
    departures = call(
        functools.partial(departures_kernel, cap, chunk),
        sds((owners * cap, channels), BF16),
        (arrived, column, pick, evolved, sigma.reshape(1, channels)),
        vmem=32,
    )
    order = sorted(range(groups), key=lambda k: -min(k, groups - k))
    gradients = call(
        functools.partial(adjoint_kernel, order, quarter),
        [sds((-(-width // 32) * 32, quarter), BF16)] * groups,
        (ids, departures, first, second, w1, w_second, w_third),
        vmem=32,
        cost_estimate=pl.CostEstimate(flops=8 * 10**9, bytes_accessed=4 * 10**6, transcendentals=0),
    )
    shares = [
        lax.ppermute(part, AXES, [(number[p], at_home(p, (p[4] + k) % groups)) for p in everyone])
        for k, part in zip(order, gradients)
    ]
    total = shares[0]
    for share in shares[1:-1]:
        total = call(
            add_kernel,
            sds(share.shape, F32),
            (total, share),
            vmem=24,
            cost_estimate=pl.CostEstimate(flops=10**10, bytes_accessed=10**6, transcendentals=0),
        )
    return call(total_kernel, sds((width, quarter), F32), (total, shares[-1]), vmem=24).T


def solution(mesh):
    grid, chan = mesh.devices.shape
    places = 4
    near = jax.sharding.Mesh(mesh.devices.reshape(places, 2, grid // (4 * places), 2, chan), AXES)
    whole = P((*GRID, "chan"), None)
    in_specs = (P(GRID, None), whole, P((*GRID, "chan")), whole, P(), whole, P(), P(), P())
    return jax.shard_map(on_device, mesh=near, in_specs=in_specs, out_specs=whole, check_vma=False)
```

```python
import functools
import itertools
import math

import jax
import jax.numpy as jnp
from jax import lax
from jax.experimental import pallas as pl
from jax.experimental.pallas import tpu as pltpu
from jax.sharding import PartitionSpec as P

LANES = 128
BASE = 32
AXES = ("zhi", "zlo", "y", "core", "chan")
GROUP = AXES[1:]
GRID = AXES[:-1]


def home(place, places):
    zhi, zlo, y, core, chan = place
    shift = (chan + 2 * core) % places
    return (zhi + shift) % places, zlo ^ int(shift == places // 2), y, core


def devices(sizes):
    return list(itertools.product(*(range(n) for n in sizes)))
F32 = jnp.float32
BF16 = jnp.bfloat16
NT = (((1,), (1,)), ((), ()))


def iota(shape, axis):
    return lax.broadcasted_iota(jnp.int32, shape, axis)


def nn(a, b):
    return jnp.dot(a, b, preferred_element_type=F32)


def nt(a, b):
    return lax.dot_general(a, b, NT, preferred_element_type=F32)


def call(kernel, out, args, vmem=48, **kw):
    return pl.pallas_call(
        kernel,
        out_shape=out,
        compiler_params=pltpu.CompilerParams(vmem_limit_bytes=vmem * 2**20),
        **kw,
    )(*args)


def flat(a):
    return jnp.concatenate([a[r : r + 1, :] for r in range(a.shape[0])], axis=1)


def push_kernel(
    owners,
    cap,
    chunk,
    target_hbm,
    offset_hbm,
    observed_hbm,
    flags_hbm,
    out_hbm,
    target_ref,
    offset_ref,
    observed_ref,
    flags_ref,
    data,
    staged,
    sems,
    out_sems,
):
    pairs = (
        (target_hbm, target_ref),
        (offset_hbm, offset_ref),
        (observed_hbm, observed_ref),
        (flags_hbm, flags_ref),
    )
    gets = [pltpu.make_async_copy(src, dst, sems.at[k]) for k, (src, dst) in enumerate(pairs)]
    for get in gets:
        get.start()
    gets[0].wait()
    gets[1].wait()
    tiles = target_ref.shape[0]
    count = tiles * LANES
    channels = observed_ref.shape[1]
    owner = flat(target_ref[...])
    places = lax.axis_size("zhi")
    near = owners // places
    shift = (owner // near - lax.axis_index("zhi") + places) & (places - 1)
    ring = (shift - 2 * (owner & 1) + places) & (places - 1)
    swap = jnp.where(shift == places // 2, near // 2, 0)
    target = ((owner & (near - 1)) ^ swap) * places + ring
    offset = flat(offset_ref[...])
    hot = jnp.where(iota((owners, count), 0) == target, 1.0, 0.0)
    upper = jnp.where(iota((256, 256), 0) <= iota((256, 256), 1), 1.0, 0.0).astype(BF16)
    carry = jnp.zeros((owners, 1), F32)
    slots = []
    for b in range(count // 256):
        part = hot[:, b * 256 : (b + 1) * 256]
        seen = nn(part.astype(BF16), upper) + carry
        carry = seen[:, 255:256]
        slots.append(jnp.sum(part * (seen - 1.0), axis=0, keepdims=True))
    slot = jnp.concatenate(slots, axis=1)
    place = target * cap + slot.astype(jnp.int32)
    high = offset // BASE
    low = offset - high * BASE
    at_slot = jnp.where((iota((LANES, count), 0) & (cap - 1)).astype(F32) == slot, 1.0, 0.0)
    hot = hot.astype(BF16)
    pair = jnp.concatenate([at_slot * (high + 1).astype(F32), at_slot * low.astype(F32)], axis=0)
    pair = nt(hot, pair.astype(BF16))
    high, low = pair[:, :LANES] - 1.0, pair[:, LANES:]

    gets[2].wait()
    data[:, :channels] = observed_ref[...].astype(BF16)
    gets[3].wait()
    data[:, channels:] = flags_ref[...].astype(F32).astype(BF16)
    parts = 2 * channels // LANES
    puts = []
    for k, s in enumerate(range(0, owners, chunk)):
        put = jnp.where(place - s * cap == iota((chunk * cap, count), 0), 1.0, 0.0).astype(BF16)
        rows = nn(put, data[...]).astype(BF16).reshape(chunk, cap, 2 * channels)
        for j in range(parts):
            staged[s : s + chunk, j * cap : (j + 1) * cap, :] = rows[:, :, j * LANES : (j + 1) * LANES]
        digits = jnp.where(
            iota((chunk, 8, LANES), 1) == 0,
            high[s : s + chunk, :].reshape(chunk, 1, LANES),
            low[s : s + chunk, :].reshape(chunk, 1, LANES),
        )
        staged[s : s + chunk, parts * cap :, :] = digits.astype(BF16)
        puts.append(
            pltpu.make_async_copy(
                staged.at[pl.ds(s, chunk)], out_hbm.at[pl.ds(s, chunk)], out_sems.at[k]
            )
        )
        puts[-1].start()
    for put in puts:
        put.wait()


def forward_kernel(table_ref, w1_ref, w2_ref, w3_ref, evolved_ref, first_ref, second_ref):
    first = jnp.tanh(nn(table_ref[...], w1_ref[...])).astype(BF16)
    second = jnp.tanh(nn(first, w2_ref[...])).astype(BF16)
    first_ref[...] = first
    second_ref[...] = second
    evolved_ref[...] = nn(second, w3_ref[...]).astype(BF16)


def one_hot(cap, column, sources, cols):
    wide = iota((cap, cols), 1).astype(F32)
    picks = [jnp.where(column[:, s : s + 1] == wide, 1.0, 0.0).astype(BF16) for s in sources]
    return jnp.concatenate(picks, axis=0)


def decode_kernel(cap, chunk, parts, arrived_ref, ids_ref, column_ref, pick_ref):
    sources = arrived_ref.shape[0]
    digits = arrived_ref[:, 2 * parts * cap :, :].reshape(sources * 8, LANES)
    row = iota((sources, sources * 8), 1) - 8 * iota((sources, sources * 8), 0)
    high = nn(jnp.where(row == 0, 1.0, 0.0).astype(BF16), digits)
    low = nn(jnp.where(row == 1, 1.0, 0.0).astype(BF16), digits)
    per = LANES // cap
    mine = iota((sources, LANES), 1) // cap == iota((sources, LANES), 0) % per
    gather = jnp.where(
        iota((sources // per, sources), 1) // per == iota((sources // per, sources), 0), 1.0, 0.0
    ).astype(BF16)
    spread = lambda a: nn(gather, jnp.where(mine, a, 0.0).astype(BF16))
    ids_ref[...] = (spread(high) * BASE + spread(low)).astype(jnp.int32)
    column = (high * BASE + low).T[:cap, :]
    column_ref[...] = column
    count, cols = pick_ref.shape
    for s in range(0, count // cap, chunk):
        pick_ref[s * cap : (s + chunk) * cap, :] = one_hot(cap, column, range(s, s + chunk), cols)


def departures_kernel(
    cap, chunk, arrived_ref, column_ref, pick_ref, evolved_ref, sigma_ref, out_ref
):
    sources = arrived_ref.shape[0]
    cols, channels = evolved_ref.shape
    parts = channels // LANES
    column = column_ref[...]
    inverse = 1.0 / sigma_ref[...]
    for s in range(0, sources, chunk):
        if s * cap < pick_ref.shape[0]:
            pick = pick_ref[s * cap : (s + chunk) * cap, :]
        else:
            pick = one_hot(cap, column, range(s, s + chunk), cols)
        evolved = nn(pick, evolved_ref[...])
        for j in range(parts):
            lanes = slice(j * LANES, (j + 1) * LANES)
            take = lambda k: arrived_ref[s : s + chunk, k * cap : (k + 1) * cap, :].reshape(
                chunk * cap, LANES
            ).astype(F32)
            departure = (evolved[:, lanes] - take(j)) * inverse[:, lanes]
            weighted = take(parts + j) * jnp.clip(departure, -1.5, 1.5) * inverse[:, lanes]
            out_ref[s * cap : (s + chunk) * cap, lanes] = weighted.astype(BF16)


def adjoint_kernel(
    shifts, quarter, ids_ref, departures_ref, first_ref, second_ref, w1_ref, w2_ref, w3_ref, *outs
):
    groups = len(shifts)
    each = range(groups)
    which = [lax.rem(lax.axis_index("chan") + k, groups) * quarter for k in shifts]
    rows = [pl.ds(pl.multiple_of(start, quarter), quarter) for start in which]
    ids = flat(ids_ref[...])
    grad_second, grad_first = [], []
    put = [
        jnp.where(ids - which[k] == iota((quarter, ids.shape[1]), 0), 1.0, 0.0).astype(BF16)
        for k in each
    ]
    sums = nn(jnp.concatenate(put, axis=0), departures_ref[...]).astype(BF16)
    total = [sums[k * quarter : (k + 1) * quarter, :] for k in each]
    for k in each:
        second = second_ref[rows[k], :].astype(F32)
        grad_second.append((nt(total[k], w3_ref[...]) * (1.0 - second * second)).astype(BF16))
    for k in each:
        first = first_ref[rows[k], :].astype(F32)
        grad_first.append((nt(grad_second[k], w2_ref[...]) * (1.0 - first * first)).astype(BF16))
    for k, out_ref in enumerate(outs):
        out_ref[...] = nt(w1_ref[: out_ref.shape[0], :], grad_first[k]).astype(BF16)


def add_kernel(so_far_ref, part_ref, out_ref):
    out_ref[...] = so_far_ref[...].astype(F32) + part_ref[...].astype(F32)


def total_kernel(so_far_ref, part_ref, out_ref):
    total = so_far_ref[...] + part_ref[...].astype(F32)
    out_ref[...] = total[: out_ref.shape[0], :]


def on_device(
    profiles, owner_block, column_offset, observed, sigma, qc_flags, w_first, w_second, w_third
):
    sizes = tuple(lax.axis_size(name) for name in AXES)
    owners = math.prod(sizes[:-1])
    places, groups = sizes[0], sizes[-1]
    everyone = devices(sizes)
    number = {place: i for i, place in enumerate(everyone)}
    rows = owner_block.shape[0]
    cap = 2 * rows // owners
    cols, width = profiles.shape
    hidden, channels = w_third.shape
    quarter = cols // groups
    tiles = rows // LANES
    chunk = 16
    few = 8
    sds = jax.ShapeDtypeStruct
    far = pl.BlockSpec(memory_space=pltpu.HBM)

    def at_home(place, chan):
        return number[(*home(place, places), chan)]

    fetched = lax.ppermute(profiles.T, AXES, [(at_home(p, p[4]), number[p]) for p in everyone])

    bundle = sds((owners, 2 * channels // LANES * cap + 8, LANES), BF16)
    pushed = call(
        functools.partial(push_kernel, owners, cap, few),
        bundle,
        (owner_block.reshape(tiles, LANES), column_offset.reshape(tiles, LANES), observed, qc_flags),
        vmem=62,
        in_specs=[far] * 4,
        out_specs=far,
        scratch_shapes=[
            pltpu.VMEM((tiles, LANES), jnp.int32),
            pltpu.VMEM((tiles, LANES), jnp.int32),
            pltpu.VMEM((rows, channels), F32),
            pltpu.VMEM((rows, channels), jnp.int32),
            pltpu.VMEM((rows, 2 * channels), BF16),
            pltpu.VMEM(bundle.shape, BF16),
            pltpu.SemaphoreType.DMA((4,)),
            pltpu.SemaphoreType.DMA((owners // few,)),
        ],
    )
    arrived = lax.all_to_all(pushed, GROUP, split_axis=0, concat_axis=0, tiled=True)

    padded = -(-width // LANES) * LANES
    wide = lambda a, axis: jnp.pad(a, [(0, padded - width) if k == axis else (0, 0) for k in (0, 1)])
    w1 = wide(w_first, 0)
    evolved, first, second = call(
        forward_kernel,
        (sds((cols, channels), BF16), sds((cols, hidden), BF16), sds((cols, hidden), BF16)),
        (wide(fetched.T, 1), w1, w_second, w_third),
        vmem=24,
        cost_estimate=pl.CostEstimate(flops=10**11, bytes_accessed=4 * 10**6, transcendentals=10**6),
    )

    ids, column, pick = call(
        functools.partial(decode_kernel, cap, chunk, channels // LANES),
        (
            sds((owners * cap // LANES, LANES), jnp.int32),
            sds((cap, owners), F32),
            sds((2 * chunk * cap, cols), BF16),
        ),
        (arrived,),
        vmem=32,
        cost_estimate=pl.CostEstimate(flops=2 * 10**9, bytes_accessed=10**5, transcendentals=0),
    )
    departures = call(
        functools.partial(departures_kernel, cap, chunk),
        sds((owners * cap, channels), BF16),
        (arrived, column, pick, evolved, sigma.reshape(1, channels)),
        vmem=32,
    )
    order = sorted(range(groups), key=lambda k: -min(k, groups - k))
    gradients = call(
        functools.partial(adjoint_kernel, order, quarter),
        [sds((-(-width // 32) * 32, quarter), BF16)] * groups,
        (ids, departures, first, second, w1, w_second, w_third),
        vmem=32,
        cost_estimate=pl.CostEstimate(flops=8 * 10**9, bytes_accessed=4 * 10**6, transcendentals=0),
    )
    shares = [
        lax.ppermute(part, AXES, [(number[p], at_home(p, (p[4] + k) % groups)) for p in everyone])
        for k, part in zip(order, gradients)
    ]
    total = shares[0]
    for share in shares[1:-1]:
        total = call(
            add_kernel,
            sds(share.shape, F32),
            (total, share),
            vmem=24,
            cost_estimate=pl.CostEstimate(flops=10**10, bytes_accessed=10**6, transcendentals=0),
        )
    return call(total_kernel, sds((width, quarter), F32), (total, shares[-1]), vmem=24).T


def solution(mesh):
    grid, chan = mesh.devices.shape
    places = 4
    near = jax.sharding.Mesh(mesh.devices.reshape(places, 2, grid // (4 * places), 2, chan), AXES)
    whole = P((*GRID, "chan"), None)
    in_specs = (P(GRID, None), whole, P((*GRID, "chan")), whole, P(), whole, P(), P(), P())
    return jax.shard_map(on_device, mesh=near, in_specs=in_specs, out_specs=whole, check_vma=False)
```
